256 devices in a mesh: grp: 32 (over z, x_lo, core), tp: 8 (over y, x_hi).
Axes of the slice: x: 4 (x_hi: 2, x_lo: 2; x = x_hi * 2 + x_lo), y: 4, z: 8, core: 2. Of those that a mesh axis runs over, the one named last changes fastest.
Arguments:
- queries: bfloat16 [8192, 4096], P('grp', 'tp'), may hold values from -60 to 60
- key_rows: bfloat16 [8192, 1024], P('grp', 'tp'), may hold values from -6 to 6
- value_rows: bfloat16 [8192, 1024], P('grp', 'tp'), may hold values from -6 to 6
- out_weight: bfloat16 [4096, 8192], P('tp'), may hold values from -1.5 to 1.5
- block_order: int32 [32], replicated, may hold values from 0 to 31, each once
- page_owner: int32 [512, 1], replicated, may hold values from 0 to 31, as said below
Outputs:
- attention_out: bfloat16 [8192, 8192], P('grp', 'tp')
- page_cache: bfloat16 [2048, 16, 2048], P('grp', None, 'tp')
The draws below stay inside these ranges and needn't reach their ends.
Inputs may be any that keep to these rules, and one draw needn't show every extreme that they name: `page_owner`: the 16 pages of one device name each owner at most 2 times; one owner is named exactly 2 times by every device.
All inputs are finite; a program needn't handle non-finite values.
Results may differ from the reference program's by a relative error of at most 0.017.
Values may be sent and summed in bfloat16 or wider, within the bound.
A program may use at most 64 MiB of HBM per device.

```python
import jax
import jax.numpy as jnp
from jax import lax

D = 8192
HEAD_DIM = 128
QPK = 4
ROWS_DEV = 256
PAGE = 16
MOST = 2
KV_HEADS = 8
HEADS = 32
TOKENS = 8192
PAGES_DEV = 16
NPAGES = 512
SLOTS = 64
N_GRP = 32


def key_parts(key):
    normal_part = jax.random.normal(jax.random.fold_in(key, 11), (TOKENS, KV_HEADS, HEAD_DIM), jnp.float32)
    return jnp.clip(normal_part, -6.0, 6.0)


def draw_key_rows(key, part):
    normal_part = key_parts(key)
    chosen = normal_part
    return chosen.reshape(TOKENS, KV_HEADS * HEAD_DIM).astype(jnp.bfloat16)


def draw_queries(key, part):
    key = jax.random.fold_in(key, 5)
    fresh_shape = (TOKENS, KV_HEADS, QPK, HEAD_DIM)
    fresh = jnp.clip(1.5 * jax.random.normal(key, fresh_shape, jnp.float32), -9.0, 9.0)
    return fresh.reshape(TOKENS, HEADS * HEAD_DIM).astype(jnp.bfloat16)


def draw_page_owner(key, part):
    key = jax.random.fold_in(key, 7)
    hot_owner = jax.random.randint(jax.random.fold_in(key, 1), (), 0, N_GRP)
    others = (hot_owner + 1 + jnp.arange(N_GRP - 1)) % N_GRP
    owner_pool = jnp.concatenate([others, others]).astype(jnp.int32)

    def one_block(block_key):
        first_key, second_key = jax.random.split(block_key)
        picked = jax.random.permutation(first_key, owner_pool)[:PAGES_DEV - MOST]
        block_row = jnp.concatenate([jnp.zeros((MOST,), jnp.int32) + hot_owner, picked])
        return jax.random.permutation(second_key, block_row)
    block_keys = jax.random.split(jax.random.fold_in(key, 2), N_GRP)
    return jax.vmap(one_block)(block_keys).reshape(N_GRP * PAGES_DEV, 1).astype(jnp.int32)


def shard_levels(rng, dims, shards, least, high):
    factor_of, own = 1.0, jax.random.fold_in(rng, 6)
    for dim, shards_of in shards:
        draws = jnp.exp(jax.random.uniform(jax.random.fold_in(own, dim), (shards_of,), jnp.float32, least / len(shards), high / len(shards)))
        factor_of = factor_of * jnp.repeat(draws, dims[dim] // shards_of).reshape([-1 if axis == dim else 1 for axis in range(len(dims))])
    return factor_of


def bell_draw(rng, shape, scale, most, cuts=(), kind=jnp.bfloat16):
    factor_of = shard_levels(rng, shape, cuts, -0.22, 0.18) if cuts else 1.0
    result = jax.random.normal(rng, shape, jnp.float32) * scale * factor_of
    return jnp.minimum(jnp.maximum(result, -most), most).astype(kind)


def setup_inputs(seed: int = 0) -> dict:
    splits = jax.random.split(jax.random.key(seed), 7)
    queries = draw_queries(jax.random.fold_in(splits[6], 71), 0)
    key_rows = draw_key_rows(jax.random.fold_in(splits[6], 71), 0)
    value_rows = bell_draw(splits[2], (TOKENS, KV_HEADS * HEAD_DIM), 1.0, 6.0, ((0, 32), (1, 8)))
    out_weight = bell_draw(splits[3], (HEADS * HEAD_DIM, D), (16.0 / (HEADS * HEAD_DIM) ** 0.5), 1.5, ((0, 8),))
    block_order = jax.random.permutation(splits[4], N_GRP).astype(jnp.int32)
    page_owner = draw_page_owner(jax.random.fold_in(splits[6], 71), 0)
    return dict(queries=queries, key_rows=key_rows, value_rows=value_rows, out_weight=out_weight, block_order=block_order, page_owner=page_owner)


masked_score = -1e30


def reference(queries, key_rows, value_rows, out_weight, block_order, page_owner):
    score_scale = HEAD_DIM ** -0.5
    row_ids = jnp.arange(TOKENS, dtype=jnp.int32)
    where_pos = block_order[row_ids // ROWS_DEV] * ROWS_DEV + row_ids % ROWS_DEV
    key_heads = key_rows.astype(jnp.float32).reshape(TOKENS, KV_HEADS, HEAD_DIM)
    value_heads = value_rows.astype(jnp.float32).reshape(TOKENS, KV_HEADS, HEAD_DIM)

    def one_block(block_index):
        first_row = block_index * ROWS_DEV
        query_block = lax.dynamic_slice_in_dim(queries, first_row, ROWS_DEV, 0).astype(jnp.float32)
        query_block = query_block.reshape(ROWS_DEV, KV_HEADS, QPK, HEAD_DIM)
        query_pos = lax.dynamic_slice_in_dim(where_pos, first_row, ROWS_DEV, 0)
        scores = jnp.einsum("cgpd,tgd->gpct", query_block, key_heads) * score_scale
        allowed = where_pos[None, None, None, :] <= query_pos[None, None, :, None]
        scores = jnp.where(allowed, scores, masked_score)
        row_peak = jnp.max(scores, axis=-1, keepdims=True)
        exponent = jnp.where(allowed, jnp.exp(scores - row_peak), 0.0)
        row_total = jnp.sum(exponent, axis=-1)
        weights = lax.optimization_barrier(exponent.astype(jnp.bfloat16)).astype(jnp.float32)
        combined = jnp.einsum("gpct,tgd->cgpd", weights, value_heads)
        attended = combined / jnp.transpose(row_total, (2, 0, 1))[..., None]
        return attended.reshape(ROWS_DEV, HEADS * HEAD_DIM).astype(jnp.bfloat16)

    attended = lax.map(one_block, jnp.arange(N_GRP, dtype=jnp.int32))
    attended = attended.reshape(TOKENS, HEADS * HEAD_DIM)
    group_cols = QPK * HEAD_DIM
    summed = jnp.zeros((TOKENS, D), jnp.float32)
    for head_group in range(KV_HEADS):
        part_term = jnp.dot(attended[:, head_group * group_cols:(head_group + 1) * group_cols],
                            out_weight[head_group * group_cols:(head_group + 1) * group_cols],
                            preferred_element_type=jnp.float32)
        summed = summed + lax.optimization_barrier(part_term.astype(jnp.bfloat16)).astype(jnp.float32)
    attention_out = summed.astype(jnp.bfloat16)

    page_rows = jnp.stack([key_rows.reshape(TOKENS, KV_HEADS, HEAD_DIM),
                           value_rows.reshape(TOKENS, KV_HEADS, HEAD_DIM)], axis=2)
    page_rows = page_rows.reshape(NPAGES, PAGE, KV_HEADS * 2 * HEAD_DIM)
    owners = page_owner[:, 0].astype(jnp.int32)
    owner_hits = (owners[:, None] == jnp.arange(N_GRP, dtype=jnp.int32)[None, :]).astype(jnp.int32)
    before = jnp.cumsum(owner_hits, axis=0) - owner_hits
    page_rank = jnp.sum(before * owner_hits, axis=1).astype(jnp.int32)
    slot_index = owners * SLOTS + page_rank
    page_cache = jnp.zeros((N_GRP * SLOTS, PAGE, KV_HEADS * 2 * HEAD_DIM), key_rows.dtype)
    page_cache = page_cache.at[slot_index].set(page_rows)
    return attention_out, page_cache
```

```python
import functools

import jax
import jax.numpy as jnp
from jax import lax
from jax.experimental import pallas as pl
from jax.experimental.pallas import tpu as pltpu
from jax.sharding import PartitionSpec as P

MESH = pl.DeviceIdType.MESH
HEAD = 128
QPK = 4
ROWS = 256
PAGE = 16
COLS = 1024
SLOTS = 64
NPAGES = 512
NEG = -1e30
SCALE2 = 128.0 ** -0.5 * 1.4426950408889634

Z_SET = (1, 2, 4, 5, 7, 8, 9, 11, 12, 14, 15)
X_SET = (3, 6, 10, 13)
N_SET = 16

GROUP = 32
Y_FIRST = 5
X_FIRST = 3


def plus_slot(r):
    return 4 * Z_SET[r]


def minus_slot(r):
    return 4 * Z_SET[r] + 1


def x_slot(i):
    return 4 * X_SET[i // 2] + i % 2


def half_blocks(z, xl, c):
    def index(dz, other, flip):
        return lax.rem(z + dz + 8, 8) * 4 + (1 - xl if other else xl) * 2 + (1 - c if flip else c)

    found = []
    for flip in (0, 1):
        at = 2 * flip
        found += [(at, index(0, 0, flip), 0), (at + 1, index(0, 0, flip), 1)]
        for r in range(11):
            d = r // 3 + 1
            if r < 9:
                half, other = ((0, 0), (1, 0), (0, 1))[r % 3]
            else:
                half, other = (0, r - 9)
            found.append((plus_slot(r) + at, index(-d, other, flip), half))
            if r < 9:
                half, other = ((1, 0), (0, 0), (0, 1))[r % 3]
            else:
                half, other = (1, r - 9)
            found.append((minus_slot(r) + at, index(d, other, flip), half))
        for i, (dz, half) in enumerate(((0, 0), (0, 1), (1, 1), (-1, 1), (2, 1), (-2, 1), (3, 1), (-3, 1))):
            found.append((x_slot(i) + at, index(dz, 1, flip), half))
    return found


def kernel(order_ref, owner_ref, q_hbm, k_hbm, v_hbm, w_hbm, out_ref, pages_ref,
           kv, q_raw, qx, top, acc, att, w, part, uy, ux, wx, wy, table_v, table_s, place, holder,
           load_sem, w_sem, z_ssem, z_rsem, x_ssem, x_rsem, d_ssem, d_rsem,
           uy_ssem, uy_rsem, ux_ssem, ux_rsem, wx_ssem, wx_rsem, wy_ssem, wy_rsem):
    grp, tp = lax.axis_index("grp"), lax.axis_index("tp")
    z, xl, c = grp // 4, lax.rem(grp // 2, 2), lax.rem(grp, 2)
    y, xh = tp // 2, lax.rem(tp, 2)

    def at_grp(z_to, xl_to, c_to):
        return (z_to * 4 + xl_to * 2 + c_to, tp)

    z_up = at_grp(lax.rem(z + 1, 8), xl, c)
    z_down = at_grp(lax.rem(z + 7, 8), xl, c)
    x_near = at_grp(z, 1 - xl, c)
    core = at_grp(z, xl, 1 - c)
    y_up = (grp, lax.rem(y + 1, 4) * 2 + xh)
    y_down = (grp, lax.rem(y + 3, 4) * 2 + xh)
    x_far = (grp, y * 2 + 1 - xh)

    loads = []
    for half in range(2):
        for ref, lane in ((k_hbm, 0), (v_hbm, HEAD)):
            loads.append(pltpu.make_async_copy(
                ref.at[pl.ds(8 * half, 8)], kv.at[pl.ds(8 * half, 8), :, pl.ds(lane, HEAD)],
                load_sem.at[len(loads)]))
    load_q = pltpu.make_async_copy(q_hbm, q_raw, load_sem.at[4])
    load_w = pltpu.make_async_copy(w_hbm, w, w_sem)
    for load in loads:
        load.start()
    load_q.start()
    load_w.start()

    barrier = pltpu.get_barrier_semaphore()
    for near in (z_up, z_down, x_near, core, y_up, y_down, x_far):
        pl.semaphore_signal(barrier, inc=1, device_id=near, device_id_type=MESH)

    here = order_ref[grp]
    for slot, block, half in half_blocks(z, xl, c):
        place[2 * block + half] = slot + 0 * grp
        holder[slot] = block

    for load in loads:
        load.wait()
    pl.semaphore_wait(barrier, 7)

    sent = []

    def remote(src, dst, ssem, rsem, to):
        return pltpu.make_async_remote_copy(src_ref=src, dst_ref=dst, send_sem=ssem, recv_sem=rsem,
                                            device_id=to, device_id_type=MESH)

    def slots(first, count=1):
        return kv.at[pl.ds(8 * first, 8 * count)]

    def plus(r, src):
        return remote(slots(src), slots(plus_slot(r)), z_ssem.at[0, r], z_rsem.at[0, r], z_up)

    def minus(r, src):
        return remote(slots(src), slots(minus_slot(r)), z_ssem.at[1, r], z_rsem.at[1, r], z_down)

    def cross(i, src):
        return remote(slots(src), slots(x_slot(i)), x_ssem.at[i], x_rsem.at[i], x_near)

    def twin(k):
        return remote(slots(4 * k, 2), slots(4 * k + 2, 2), d_ssem.at[k], d_rsem.at[k], core)

    def begin(make, *which):
        make(*which).start()
        sent.append((make, which))

    begin(cross, 0, 0)
    begin(plus, 0, 0)
    begin(minus, 0, 1)
    begin(twin, 0)
    begin(cross, 1, 1)
    begin(plus, 1, 1)
    begin(minus, 1, 0)

    def z_step(r):
        plus(r, 0).wait_recv()
        minus(r, 0).wait_recv()
        if r <= 6:
            begin(plus, r + 3, plus_slot(r))
            begin(minus, r + 3, minus_slot(r))
        if r == 8:
            begin(plus, 10, plus_slot(8))
        if r % 3 == 0 and r <= 6:
            begin(cross, 2 + 2 * (r // 3), minus_slot(r))
        if r % 3 == 1 and r <= 7:
            begin(cross, 3 + 2 * (r // 3), plus_slot(r))
        begin(twin, Z_SET[r])

    def x_step(i):
        cross(i, 0).wait_recv()
        if i == 0:
            begin(plus, 2, x_slot(0))
            begin(minus, 2, x_slot(0))
        if i == 6:
            begin(minus, 10, x_slot(6))
        if i % 2 == 1:
            begin(twin, X_SET[i // 2])

    before = {
        1: (("z", 0), ("z", 1), ("x", 1)),
        2: (("z", 2),),
        4: (("z", 3), ("x", 2)),
        5: (("z", 4), ("x", 3)),
        7: (("z", 5),),
        8: (("z", 6), ("x", 4)),
        9: (("z", 7), ("x", 5)),
        11: (("z", 8), ("x", 6)),
        12: (("z", 9), ("x", 7)),
        14: (("z", 10),),
    }

    def softmax_step(k, first):
        block = kv[pl.ds(32 * k, 32)].reshape(512, 2 * HEAD)
        rows = []
        for j in range(4):
            seen = order_ref[holder[4 * k + j]] < here
            if first and j < 2:
                seen = True
            rows.append(jnp.full((HEAD, HEAD), jnp.where(seen, 0.0, NEG), jnp.float32).astype(jnp.bfloat16))
        keys = jnp.concatenate([block[:, :HEAD], jnp.concatenate(rows, axis=0)], axis=1)
        values = jnp.concatenate([block[:, HEAD:], jnp.ones((512, HEAD), jnp.bfloat16)], axis=1)
        for h in range(QPK):
            scores = lax.dot_general(qx[h], keys, (((1,), (1,)), ((), ())), preferred_element_type=jnp.float32)
            tiles = [scores[:, HEAD * j:HEAD * (j + 1)] for j in range(4)]
            if first:
                row = lax.broadcasted_iota(jnp.int32, (ROWS, HEAD), 0)
                lane = lax.broadcasted_iota(jnp.int32, (ROWS, HEAD), 1)
                for j in range(2):
                    tiles[j] = jnp.where(lane + HEAD * j <= row, tiles[j], NEG)
            peak = jnp.max(jnp.maximum(jnp.maximum(tiles[0], tiles[1]), jnp.maximum(tiles[2], tiles[3])),
                           axis=1, keepdims=True)
            if first:
                new = jnp.broadcast_to(peak, (ROWS, HEAD))
            else:
                old = top[h]
                new = jnp.maximum(old, peak)
            expo = [jnp.exp2((tile - new) * SCALE2).astype(jnp.bfloat16) for tile in tiles]
            gained = jnp.dot(jnp.concatenate(expo, axis=1), values, preferred_element_type=jnp.float32)
            top[h] = new
            if first:
                acc[h] = gained
            else:
                factor = jnp.exp2((old - new) * SCALE2)
                acc[h] = acc[h] * jnp.concatenate([factor, factor], axis=1) + gained

    load_q.wait()
    lane = lax.broadcasted_iota(jnp.int32, (ROWS, HEAD), 1)
    unit = jnp.where(lane == 0, 1.0, 0.0).astype(jnp.bfloat16)
    for h in range(QPK):
        qx[h] = jnp.concatenate([q_raw[:, HEAD * h:HEAD * (h + 1)], unit], axis=1)
    x_step(0)
    twin(0).wait_recv()
    softmax_step(0, True)

    @pl.loop(1, N_SET)
    def _(k):
        for at, events in before.items():
            @pl.when(k == at)
            def _():
                for kind, r in events:
                    (z_step if kind == "z" else x_step)(r)
        twin(k).wait_recv()
        softmax_step(k, False)

    for h in range(QPK):
        att[:, HEAD * h:HEAD * (h + 1)] = (acc[h, :, :HEAD] / acc[h, :, HEAD:]).astype(jnp.bfloat16)
    load_w.wait()

    def project(i, j):
        first = (lax.rem(y + i, 4) * 2 + (1 - xh if j else xh)) * COLS

        @pl.loop(0, 4)
        def _(n):
            at = pl.multiple_of(first + n * 256, 256)
            to = pl.multiple_of(n * 256, 256)
            part[i, j, :, pl.ds(to, 256)] = jnp.dot(
                att[...], w[:, pl.ds(at, 256)], preferred_element_type=jnp.float32).astype(jnp.bfloat16)

    def rows_of(g):
        return pl.ds(g * GROUP, GROUP)

    def near_y(g, way, n, src=None):
        i, j = ((2, 0), (1, 1), (1, 0))[n] if way == 0 else ((2, 1), (3, 0), (3, 1))[n]
        return remote(part.at[i, j, rows_of(g)], uy.at[g, way, n], uy_ssem.at[g, way, n], uy_rsem.at[g, way, n],
                      (y_up, y_down)[way])

    def far_x(g):
        return remote(part.at[0, 1, rows_of(g)], ux.at[g], ux_ssem.at[g], ux_rsem.at[g], x_far)

    def far_first(g, i):
        return remote(part.at[i, 1, rows_of(Y_FIRST + g)], wx.at[g, i], wx_ssem.at[g, i], wx_rsem.at[g, i], x_far)

    def near_last(g, way, n):
        i = (2, 1, 1)[n] if way == 0 else (2, 3, 3)[n]
        left = (0, 1, 0)[n] if way == 0 else (1, 0, 1)[n]
        return remote(part.at[i, 0, rows_of(Y_FIRST + g), pl.ds(512 * left, 512)], wy.at[g, way, n],
                      wy_ssem.at[g, way, n], wy_rsem.at[g, way, n], (y_up, y_down)[way])

    def wide(a):
        return a.astype(jnp.float32)

    def u_begin(g):
        for n in (0, 1):
            for way in (0, 1):
                begin(near_y, g, way, n)

    def u_add(g):
        for way, i, j in ((0, 1, 0), (1, 3, 1)):
            near_y(g, way, 0).wait_recv()
            part[i, j, rows_of(g)] = (wide(part[i, j, rows_of(g)]) + wide(uy[g, way, 0])).astype(jnp.bfloat16)
            begin(near_y, g, way, 2)

    def u_total(g, j):
        return wide(part[0, j, rows_of(g)]) + wide(uy[g, 0, 2 - j]) + wide(uy[g, 1, 1 + j])

    def u_cross(g):
        for way in (0, 1):
            for n in (1, 2):
                near_y(g, way, n).wait_recv()
        part[0, 1, rows_of(g)] = u_total(g, 1).astype(jnp.bfloat16)
        begin(far_x, g)

    def u_out(g):
        far_x(g).wait_recv()
        out_ref[rows_of(g)] = (u_total(g, 0) + wide(ux[g])).astype(jnp.bfloat16)

    def w_begin(g):
        for i in (2, 1, 3, 0):
            begin(far_first, g, i)

    def w_mid(g):
        at = rows_of(Y_FIRST + g)
        for i in (2, 1, 3):
            far_first(g, i).wait_recv()
            part[i, 0, at] = (wide(part[i, 0, at]) + wide(wx[g, i])).astype(jnp.bfloat16)
            if i == 2:
                begin(near_last, g, 0, 0)
                begin(near_last, g, 1, 0)
            else:
                begin(near_last, g, (1 if i == 3 else 0), 1)

    def w_add(g):
        at = rows_of(Y_FIRST + g)
        for way, i in ((0, 1), (1, 3)):
            near_last(g, way, 0).wait_recv()
            cols = pl.ds(512 * way, 512)
            part[i, 0, at, cols] = (wide(part[i, 0, at, cols]) + wide(wy[g, way, 0])).astype(jnp.bfloat16)
            begin(near_last, g, way, 2)

    def w_out(g):
        at = rows_of(Y_FIRST + g)
        far_first(g, 0).wait_recv()
        for way in (0, 1):
            for n in (1, 2):
                near_last(g, way, n).wait_recv()
        total = wide(part[0, 0, at]) + wide(wx[g, 0])
        came = [wide(wy[g, 0, 2 - left]) + wide(wy[g, 1, 1 + left]) for left in (0, 1)]
        out_ref[at] = (total + jnp.concatenate(came, axis=1)).astype(jnp.bfloat16)

    def hand_pages():
        lanes = lax.broadcasted_iota(jnp.int32, (8, 128), 1)

        def look(i, carry):
            found, count = carry
            mine = owner_ref[i] == grp
            found = jnp.where((lanes == count) & mine, i, found)
            return found, count + jnp.where(mine, 1, 0)

        found, count = lax.fori_loop(0, NPAGES, look, (jnp.zeros((8, 128), jnp.int32), 0 * grp), unroll=8)
        table_v[...] = found
        fetch = pltpu.make_async_copy(table_v, table_s, load_sem.at[5])
        fetch.start()
        fetch.wait()

        @pl.loop(0, SLOTS)
        def _(s):
            page = table_s[0, s]
            slot = place[page // 8]
            rows = kv[slot * 8 + lax.rem(page, 8)]
            pages_ref[s] = jnp.where(s < count, rows, jnp.zeros_like(rows))

    project(2, 0)
    begin(near_y, 0, 0, 0)
    project(2, 1)
    begin(near_y, 0, 1, 0)
    begin(far_first, 0, 2)
    project(1, 1)
    begin(near_y, 0, 0, 1)
    begin(far_first, 0, 1)
    project(3, 0)
    begin(near_y, 0, 1, 1)
    project(3, 1)
    begin(far_first, 0, 3)
    project(0, 1)
    begin(far_first, 0, 0)
    project(1, 0)
    u_begin(1)
    u_add(0)
    project(0, 0)
    w_begin(1)
    hand_pages()
    u_begin(2)
    u_add(1)
    u_cross(0)
    w_mid(0)
    w_begin(2)
    u_begin(3)
    u_add(2)
    u_cross(1)
    w_add(0)
    u_out(0)
    u_begin(4)
    u_add(3)
    u_cross(2)
    w_mid(1)
    u_out(1)
    w_out(0)
    u_add(4)
    u_cross(3)
    w_add(1)
    w_mid(2)
    u_out(2)
    u_cross(4)
    w_add(2)
    w_out(1)
    u_out(3)
    w_out(2)
    u_out(4)

    for make, which in sent:
        make(*which).wait_send()


def on_device(queries, key_rows, value_rows, out_weight, block_order, page_owner):
    dma = pltpu.SemaphoreType.DMA
    vmem = pltpu.VMEM
    bf16, f32, i32 = jnp.bfloat16, jnp.float32, jnp.int32
    smem_in = pl.BlockSpec(memory_space=pltpu.SMEM)
    hbm_in = pl.BlockSpec(memory_space=pl.ANY)
    vmem_out = pl.BlockSpec(memory_space=pltpu.VMEM)
    return pl.pallas_call(
        kernel,
        name="attend",
        out_shape=(jax.ShapeDtypeStruct((ROWS, COLS), bf16),
                   jax.ShapeDtypeStruct((SLOTS, PAGE, 2 * HEAD), bf16)),
        in_specs=[smem_in, smem_in, hbm_in, hbm_in, hbm_in, hbm_in],
        out_specs=(vmem_out, vmem_out),
        scratch_shapes=[
            vmem((NPAGES, PAGE, 2 * HEAD), bf16),
            vmem((ROWS, QPK * HEAD), bf16),
            vmem((QPK, ROWS, 2 * HEAD), bf16),
            vmem((QPK, ROWS, HEAD), f32),
            vmem((QPK, ROWS, 2 * HEAD), f32),
            vmem((ROWS, QPK * HEAD), bf16),
            vmem((QPK * HEAD, 8 * COLS), bf16),
            vmem((4, 2, ROWS, COLS), bf16),
            vmem((Y_FIRST, 2, 3, GROUP, COLS), bf16),
            vmem((Y_FIRST, GROUP, COLS), bf16),
            vmem((X_FIRST, 4, GROUP, COLS), bf16),
            vmem((X_FIRST, 2, 3, GROUP, COLS // 2), bf16),
            vmem((8, 128), i32),
            pltpu.SMEM((8, 128), i32),
            pltpu.SMEM((64,), i32),
            pltpu.SMEM((64,), i32),
            dma((6,)), dma,
            dma((2, 11)), dma((2, 11)), dma((8,)), dma((8,)), dma((N_SET,)), dma((N_SET,)),
            dma((Y_FIRST, 2, 3)), dma((Y_FIRST, 2, 3)), dma((Y_FIRST,)), dma((Y_FIRST,)),
            dma((X_FIRST, 4)), dma((X_FIRST, 4)), dma((X_FIRST, 2, 3)), dma((X_FIRST, 2, 3)),
        ],
        compiler_params=pltpu.CompilerParams(
            collective_id=0, has_side_effects=True, vmem_limit_bytes=56 * 2**20),
    )(block_order, page_owner.reshape(NPAGES), queries,
      key_rows.reshape(PAGE, PAGE, HEAD), value_rows.reshape(PAGE, PAGE, HEAD), out_weight)


def solution(mesh):
    placed = (P("grp", "tp"), P("grp", "tp"), P("grp", "tp"), P("tp", None), P(), P())
    return jax.shard_map(
        on_device,
        mesh=mesh,
        in_specs=placed,
        out_specs=(P("grp", "tp"), P("grp", None, "tp")),
        check_vma=False,
    )
```

```python
import functools

import jax
import jax.numpy as jnp
from jax import lax
from jax.experimental import pallas as pl
from jax.experimental.pallas import tpu as pltpu
from jax.sharding import PartitionSpec as P

MESH = pl.DeviceIdType.MESH
HEAD = 128
QPK = 4
ROWS = 256
PAGE = 16
COLS = 1024
SLOTS = 64
NPAGES = 512
NEG = -1e30
SCALE2 = 128.0 ** -0.5 * 1.4426950408889634

Z_SET = (1, 3, 4, 5, 7, 8, 9, 10, 12, 13, 15)
X_SET = (2, 6, 11, 14)
N_SET = 16

Y_ROWS = (48, 48, 48)
X_ROWS = (48, 64)
Y_FIRST, X_FIRST = len(Y_ROWS), len(X_ROWS)
ORDER = (
    ("p", 2, 0), ("s", "y", 0, 0, 0), ("p", 2, 1), ("s", "y", 0, 1, 0), ("s", "x", 0, 2),
    ("p", 1, 1), ("s", "y", 0, 0, 1), ("s", "y", 1, 0, 0), ("s", "y", 1, 0, 1), ("s", "y", 2, 0, 0),
    ("s", "y", 2, 0, 1), ("s", "x", 0, 1),
    ("p", 3, 0), ("s", "y", 0, 1, 1), ("s", "y", 1, 1, 0), ("s", "y", 1, 1, 1), ("s", "y", 2, 1, 0),
    ("s", "y", 2, 1, 1),
    ("p", 3, 1), ("s", "x", 0, 3),
    ("p", 0, 1), ("s", "x", 0, 0), ("s", "x", 1, 2), ("s", "x", 1, 1), ("s", "x", 1, 3), ("s", "x", 1, 0),
    ("p", 1, 0), ("p", 0, 0),
    ("ua", 0, 0), ("ua", 0, 1), ("wm", 0, 2), ("pages", 0), ("pages", 1), ("wm", 0, 1), ("pages", 2),
    ("ua", 1, 0), ("ua", 1, 1), ("wm", 0, 3), ("pages", 3), ("ua", 2, 0), ("ua", 2, 1),
    ("wm", 1, 2), ("wm", 1, 1), ("uc", 0), ("wa", 0, 0), ("wa", 0, 1), ("wm", 1, 3), ("uc", 1), ("uc", 2),
    ("wa", 1, 0), ("uo", 0), ("wa", 1, 1), ("uo", 1), ("wo", 0), ("wo", 1), ("uo", 2),
)


def plus_slot(r):
    return 4 * Z_SET[r]


def minus_slot(r):
    return 4 * Z_SET[r] + 1


def x_slot(i):
    return 4 * X_SET[i // 2] + i % 2


def half_blocks(z, xl, c):
    def index(dz, other, flip):
        return lax.rem(z + dz + 8, 8) * 4 + (1 - xl if other else xl) * 2 + (1 - c if flip else c)

    found = []
    for flip in (0, 1):
        at = 2 * flip
        found += [(at, index(0, 0, flip), 0), (at + 1, index(0, 0, flip), 1)]
        for r in range(11):
            d = r // 3 + 1
            if r < 9:
                half, other = ((0, 0), (1, 0), (0, 1))[r % 3]
            else:
                half, other = (0, r - 9)
            found.append((plus_slot(r) + at, index(-d, other, flip), half))
            if r < 9:
                half, other = ((1, 0), (0, 0), (0, 1))[r % 3]
            else:
                half, other = (1, r - 9)
            found.append((minus_slot(r) + at, index(d, other, flip), half))
        for i, (dz, half) in enumerate(((0, 0), (0, 1), (1, 1), (-1, 1), (2, 1), (-2, 1), (3, 1), (-3, 1))):
            found.append((x_slot(i) + at, index(dz, 1, flip), half))
    return found


def kernel(order_ref, owner_ref, q_hbm, k_hbm, v_hbm, w_hbm, out_ref, pages_ref,
           kv, q_raw, qx, top, acc, att, w, part, uy, ux, wx, wy, table_v, table_s, place, holder,
           load_sem, w_sem, z_ssem, z_rsem, x_ssem, x_rsem, d_ssem, d_rsem,
           uy_ssem, uy_rsem, ux_ssem, ux_rsem, wx_ssem, wx_rsem, wy_ssem, wy_rsem):
    grp, tp = lax.axis_index("grp"), lax.axis_index("tp")
    z, xl, c = grp // 4, lax.rem(grp // 2, 2), lax.rem(grp, 2)
    y, xh = tp // 2, lax.rem(tp, 2)

    def at_grp(z_to, xl_to, c_to):
        return (z_to * 4 + xl_to * 2 + c_to, tp)

    z_up = at_grp(lax.rem(z + 1, 8), xl, c)
    z_down = at_grp(lax.rem(z + 7, 8), xl, c)
    x_near = at_grp(z, 1 - xl, c)
    core = at_grp(z, xl, 1 - c)
    y_up = (grp, lax.rem(y + 1, 4) * 2 + xh)
    y_down = (grp, lax.rem(y + 3, 4) * 2 + xh)
    x_far = (grp, y * 2 + 1 - xh)

    loads = []
    for half in range(2):
        for ref, lane in ((k_hbm, 0), (v_hbm, HEAD)):
            loads.append(pltpu.make_async_copy(
                ref.at[pl.ds(8 * half, 8)], kv.at[pl.ds(8 * half, 8), :, pl.ds(lane, HEAD)],
                load_sem.at[len(loads)]))
    load_q = pltpu.make_async_copy(q_hbm, q_raw, load_sem.at[4])
    load_w = pltpu.make_async_copy(w_hbm, w, w_sem)
    for load in loads:
        load.start()
    load_q.start()
    load_w.start()

    barrier = pltpu.get_barrier_semaphore()
    for near in (z_up, z_down, x_near, core, y_up, y_down, x_far):
        pl.semaphore_signal(barrier, inc=1, device_id=near, device_id_type=MESH)

    here = order_ref[grp]
    for slot, block, half in half_blocks(z, xl, c):
        place[2 * block + half] = slot + 0 * grp
        holder[slot] = block

    for load in loads:
        load.wait()
    pl.semaphore_wait(barrier, 7)

    sent = []

    def remote(src, dst, ssem, rsem, to):
        return pltpu.make_async_remote_copy(src_ref=src, dst_ref=dst, send_sem=ssem, recv_sem=rsem,
                                            device_id=to, device_id_type=MESH)

    def slots(first, count=1):
        return kv.at[pl.ds(8 * first, 8 * count)]

    def plus(r, src):
        return remote(slots(src), slots(plus_slot(r)), z_ssem.at[0, r], z_rsem.at[0, r], z_up)

    def minus(r, src):
        return remote(slots(src), slots(minus_slot(r)), z_ssem.at[1, r], z_rsem.at[1, r], z_down)

    def cross(i, src):
        return remote(slots(src), slots(x_slot(i)), x_ssem.at[i], x_rsem.at[i], x_near)

    def twin(k):
        return remote(slots(4 * k, 2), slots(4 * k + 2, 2), d_ssem.at[k], d_rsem.at[k], core)

    def begin(make, *which):
        make(*which).start()
        sent.append((make, which))

    begin(cross, 0, 0)
    begin(plus, 0, 0)
    begin(minus, 0, 1)
    begin(twin, 0)
    begin(cross, 1, 1)
    begin(plus, 1, 1)
    begin(minus, 1, 0)

    def z_step(r):
        plus(r, 0).wait_recv()
        minus(r, 0).wait_recv()
        if r <= 6:
            begin(plus, r + 3, plus_slot(r))
            begin(minus, r + 3, minus_slot(r))
        if r == 8:
            begin(plus, 10, plus_slot(8))
        if r % 3 == 0 and r <= 6:
            begin(cross, 2 + 2 * (r // 3), minus_slot(r))
        if r % 3 == 1 and r <= 7:
            begin(cross, 3 + 2 * (r // 3), plus_slot(r))
        begin(twin, Z_SET[r])

    def x_step(i):
        cross(i, 0).wait_recv()
        if i == 0:
            begin(plus, 2, x_slot(0))
            begin(minus, 2, x_slot(0))
        if i == 6:
            begin(minus, 10, x_slot(6))
        if i % 2 == 1:
            begin(twin, X_SET[i // 2])

    before = {
        1: (("x", 0), ("z", 0), ("x", 1), ("z", 1)),
        3: (("z", 2), ("x", 2)),
        4: (("z", 3), ("x", 3)),
        5: (("z", 4),),
        6: (("z", 5),),
        7: (("z", 6), ("x", 4)),
        8: (("x", 5), ("z", 7)),
        10: (("z", 8), ("x", 6)),
        11: (("z", 9),),
        12: (("x", 7),),
        13: (("z", 10),),
    }

    def softmax_step(k, first):
        block = kv[pl.ds(32 * k, 32)].reshape(512, 2 * HEAD)
        rows = []
        for j in range(4):
            seen = order_ref[holder[4 * k + j]] < here
            if first and j < 2:
                seen = True
            rows.append(jnp.full((HEAD, HEAD), jnp.where(seen, 0.0, NEG), jnp.float32).astype(jnp.bfloat16))
        keys = jnp.concatenate([block[:, :HEAD], jnp.concatenate(rows, axis=0)], axis=1)
        values = jnp.concatenate([block[:, HEAD:], jnp.ones((512, HEAD), jnp.bfloat16)], axis=1)
        scores = [lax.dot_general(qx[h], keys, (((1,), (1,)), ((), ())), preferred_element_type=jnp.float32)
                  for h in range(QPK)]
        for h in range(QPK):
            tiles = [scores[h][:, HEAD * j:HEAD * (j + 1)] for j in range(4)]
            if first:
                row = lax.broadcasted_iota(jnp.int32, (ROWS, HEAD), 0)
                lane = lax.broadcasted_iota(jnp.int32, (ROWS, HEAD), 1)
                for j in range(2):
                    tiles[j] = jnp.where(lane + HEAD * j <= row, tiles[j], NEG)
            peak = jnp.max(jnp.maximum(jnp.maximum(tiles[0], tiles[1]), jnp.maximum(tiles[2], tiles[3])),
                           axis=1, keepdims=True)
            if first:
                new = jnp.broadcast_to(peak, (ROWS, HEAD))
            else:
                old = top[h]
                new = jnp.maximum(old, peak)
            expo = [jnp.exp2((tile - new) * SCALE2).astype(jnp.bfloat16) for tile in tiles]
            gained = jnp.dot(jnp.concatenate(expo, axis=1), values, preferred_element_type=jnp.float32)
            top[h] = new
            if first:
                acc[h] = gained
            else:
                factor = jnp.exp2((old - new) * SCALE2)
                acc[h] = acc[h] * jnp.concatenate([factor, factor], axis=1) + gained

    load_q.wait()
    lane = lax.broadcasted_iota(jnp.int32, (ROWS, HEAD), 1)
    unit = jnp.where(lane == 0, 1.0, 0.0).astype(jnp.bfloat16)
    for h in range(QPK):
        qx[h] = jnp.concatenate([q_raw[:, HEAD * h:HEAD * (h + 1)], unit], axis=1)
    twin(0).wait_recv()
    softmax_step(0, True)

    @pl.loop(1, N_SET)
    def _(k):
        for at, events in before.items():
            @pl.when(k == at)
            def _():
                for kind, r in events:
                    (z_step if kind == "z" else x_step)(r)
        twin(k).wait_recv()
        softmax_step(k, False)

    for h in range(QPK):
        att[:, HEAD * h:HEAD * (h + 1)] = (acc[h, :, :HEAD] / acc[h, :, HEAD:]).astype(jnp.bfloat16)
    load_w.wait()

    def project(i, j):
        first = (lax.rem(y + i, 4) * 2 + (1 - xh if j else xh)) * COLS

        @pl.loop(0, 4)
        def _(n):
            at = pl.multiple_of(first + n * 256, 256)
            to = pl.multiple_of(n * 256, 256)
            part[i, j, :, pl.ds(to, 256)] = jnp.dot(
                att[...], w[:, pl.ds(at, 256)], preferred_element_type=jnp.float32).astype(jnp.bfloat16)

    def u_rows(g):
        return pl.ds(sum(Y_ROWS[:g]), Y_ROWS[g])

    def w_rows(g):
        return pl.ds(sum(Y_ROWS) + sum(X_ROWS[:g]), X_ROWS[g])

    def u_near(g, way, n):
        i, j = ((2, 0), (1, 1), (1, 0))[n] if way == 0 else ((2, 1), (3, 0), (3, 1))[n]
        return remote(part.at[i, j, u_rows(g)], uy.at[g, way, n, pl.ds(0, Y_ROWS[g])],
                      uy_ssem.at[g, way, n], uy_rsem.at[g, way, n], (y_up, y_down)[way])

    def u_far(g):
        return remote(part.at[0, 1, u_rows(g)], ux.at[g, pl.ds(0, Y_ROWS[g])], ux_ssem.at[g], ux_rsem.at[g], x_far)

    def w_far(g, i):
        return remote(part.at[i, 1, w_rows(g)], wx.at[g, i, pl.ds(0, X_ROWS[g])],
                      wx_ssem.at[g, i], wx_rsem.at[g, i], x_far)

    def w_near(g, way, n):
        i = (2, 1, 1)[n] if way == 0 else (2, 3, 3)[n]
        left = (0, 1, 0)[n] if way == 0 else (1, 0, 1)[n]
        return remote(part.at[i, 0, w_rows(g), pl.ds(512 * left, 512)], wy.at[g, way, n, pl.ds(0, X_ROWS[g])],
                      wy_ssem.at[g, way, n], wy_rsem.at[g, way, n], (y_up, y_down)[way])

    def wide(a):
        return a.astype(jnp.float32)

    def u_add(g, way):
        i, j = ((1, 0), (3, 1))[way]
        u_near(g, way, 0).wait_recv()
        came = uy[g, way, 0, :Y_ROWS[g]]
        part[i, j, u_rows(g)] = (wide(part[i, j, u_rows(g)]) + wide(came)).astype(jnp.bfloat16)
        begin(u_near, g, way, 2)

    def u_total(g, j):
        size = Y_ROWS[g]
        return wide(part[0, j, u_rows(g)]) + wide(uy[g, 0, 2 - j, :size]) + wide(uy[g, 1, 1 + j, :size])

    def u_cross(g):
        for way in (0, 1):
            for n in (1, 2):
                u_near(g, way, n).wait_recv()
        part[0, 1, u_rows(g)] = u_total(g, 1).astype(jnp.bfloat16)
        begin(u_far, g)

    def u_out(g):
        u_far(g).wait_recv()
        out_ref[u_rows(g)] = (u_total(g, 0) + wide(ux[g, :Y_ROWS[g]])).astype(jnp.bfloat16)

    def w_mid(g, i):
        at = w_rows(g)
        w_far(g, i).wait_recv()
        part[i, 0, at] = (wide(part[i, 0, at]) + wide(wx[g, i, :X_ROWS[g]])).astype(jnp.bfloat16)
        if i == 2:
            begin(w_near, g, 0, 0)
            begin(w_near, g, 1, 0)
        else:
            begin(w_near, g, (1 if i == 3 else 0), 1)

    def w_add(g, way):
        at, cols = w_rows(g), pl.ds(512 * way, 512)
        i = (1, 3)[way]
        w_near(g, way, 0).wait_recv()
        came = wy[g, way, 0, :X_ROWS[g]]
        part[i, 0, at, cols] = (wide(part[i, 0, at, cols]) + wide(came)).astype(jnp.bfloat16)
        begin(w_near, g, way, 2)

    def w_out(g):
        at, size = w_rows(g), X_ROWS[g]
        w_far(g, 0).wait_recv()
        for way in (0, 1):
            for n in (1, 2):
                w_near(g, way, n).wait_recv()
        total = wide(part[0, 0, at]) + wide(wx[g, 0, :size])
        came = [wide(wy[g, 0, 2 - left, :size]) + wide(wy[g, 1, 1 + left, :size]) for left in (0, 1)]
        out_ref[at] = (total + jnp.concatenate(came, axis=1)).astype(jnp.bfloat16)

    def find_pages():
        lanes = lax.broadcasted_iota(jnp.int32, (8, 128), 1)

        def look(i, carry):
            found, count = carry
            mine = owner_ref[i] == grp
            found = jnp.where((lanes == count) & mine, i, found)
            return found, count + jnp.where(mine, 1, 0)

        found, count = lax.fori_loop(0, NPAGES, look, (jnp.zeros((8, 128), jnp.int32), 0 * grp), unroll=8)
        table_v[...] = found
        fetch = pltpu.make_async_copy(table_v, table_s, load_sem.at[5])
        fetch.start()
        fetch.wait()
        return count

    def hand_pages(first, count):
        @pl.loop(first, first + SLOTS // 4)
        def _(s):
            page = table_s[0, s]
            slot = place[page // 8]
            rows = kv[slot * 8 + lax.rem(page, 8)]
            pages_ref[s] = jnp.where(s < count, rows, jnp.zeros_like(rows))

    owned = 0
    for step, *which in ORDER:
        if step == "p":
            project(*which)
        elif step == "s":
            begin(u_near if which[0] == "y" else w_far, *which[1:])
        elif step == "pages":
            if which[0] == 0:
                owned = find_pages()
            hand_pages(which[0] * (SLOTS // 4), owned)
        else:
            {"ua": u_add, "uc": u_cross, "uo": u_out, "wm": w_mid, "wa": w_add, "wo": w_out}[step](*which)

    for make, which in sent:
        make(*which).wait_send()


def hand_over(made, paged, out, pages):
    out[...] = made[...]
    pages[...] = paged[...]


def on_device(queries, key_rows, value_rows, out_weight, block_order, page_owner):
    dma = pltpu.SemaphoreType.DMA
    vmem = pltpu.VMEM
    bf16, f32, i32 = jnp.bfloat16, jnp.float32, jnp.int32
    smem_in = pl.BlockSpec(memory_space=pltpu.SMEM)
    hbm_in = pl.BlockSpec(memory_space=pl.ANY)
    vmem_out = pl.BlockSpec(memory_space=pltpu.VMEM)
    made = pl.pallas_call(
        kernel,
        name="attend",
        out_shape=(jax.ShapeDtypeStruct((ROWS, COLS), bf16),
                   jax.ShapeDtypeStruct((SLOTS, PAGE, 2 * HEAD), bf16)),
        in_specs=[smem_in, smem_in, hbm_in, hbm_in, hbm_in, hbm_in],
        out_specs=(vmem_out, vmem_out),
        scratch_shapes=[
            vmem((NPAGES, PAGE, 2 * HEAD), bf16),
            vmem((ROWS, QPK * HEAD), bf16),
            vmem((QPK, ROWS, 2 * HEAD), bf16),
            vmem((QPK, ROWS, HEAD), f32),
            vmem((QPK, ROWS, 2 * HEAD), f32),
            vmem((ROWS, QPK * HEAD), bf16),
            vmem((QPK * HEAD, 8 * COLS), bf16),
            vmem((4, 2, ROWS, COLS), bf16),
            vmem((Y_FIRST, 2, 3, max(Y_ROWS), COLS), bf16),
            vmem((Y_FIRST, max(Y_ROWS), COLS), bf16),
            vmem((X_FIRST, 4, max(X_ROWS), COLS), bf16),
            vmem((X_FIRST, 2, 3, max(X_ROWS), COLS // 2), bf16),
            vmem((8, 128), i32),
            pltpu.SMEM((8, 128), i32),
            pltpu.SMEM((64,), i32),
            pltpu.SMEM((64,), i32),
            dma((6,)), dma,
            dma((2, 11)), dma((2, 11)), dma((8,)), dma((8,)), dma((N_SET,)), dma((N_SET,)),
            dma((Y_FIRST, 2, 3)), dma((Y_FIRST, 2, 3)), dma((Y_FIRST,)), dma((Y_FIRST,)),
            dma((X_FIRST, 4)), dma((X_FIRST, 4)), dma((X_FIRST, 2, 3)), dma((X_FIRST, 2, 3)),
        ],
        compiler_params=pltpu.CompilerParams(
            collective_id=0, has_side_effects=True, vmem_limit_bytes=56 * 2**20),
    )(block_order, page_owner.reshape(NPAGES), queries,
      key_rows.reshape(PAGE, PAGE, HEAD), value_rows.reshape(PAGE, PAGE, HEAD), out_weight)
    return pl.pallas_call(
        hand_over,
        name="hand_over",
        out_shape=tuple(jax.ShapeDtypeStruct(a.shape, a.dtype) for a in made),
        in_specs=[vmem_out, vmem_out],
        out_specs=(vmem_out, vmem_out),
    )(*made)


def solution(mesh):
    placed = (P("grp", "tp"), P("grp", "tp"), P("grp", "tp"), P("tp", None), P(), P())
    return jax.shard_map(
        on_device,
        mesh=mesh,
        in_specs=placed,
        out_specs=(P("grp", "tp"), P("grp", None, "tp")),
        check_vma=False,
    )
```

```python
import functools

import jax
import jax.numpy as jnp
from jax import lax
from jax.experimental import pallas as pl
from jax.experimental.pallas import tpu as pltpu
from jax.sharding import PartitionSpec as P

MESH = pl.DeviceIdType.MESH
HEAD = 128
QPK = 4
ROWS = 256
PAGE = 16
COLS = 1024
SLOTS = 64
NPAGES = 512
NEG = -1e30
SCALE2 = 128.0 ** -0.5 * 1.4426950408889634

Z_SET = (1, 3, 4, 5, 7, 8, 9, 10, 12, 13, 15)
X_SET = (2, 6, 11, 14)
N_SET = 16

Y_ROWS = (48, 48, 48)
X_ROWS = (48, 64)
Y_FIRST, X_FIRST = len(Y_ROWS), len(X_ROWS)
ORDER = (
    ("p", 2, 0), ("s", "y", 0, 0, 0), ("p", 2, 1), ("s", "y", 0, 1, 0), ("s", "x", 0, 2),
    ("p", 1, 1), ("s", "y", 0, 0, 1), ("s", "y", 1, 0, 0), ("s", "y", 1, 0, 1), ("s", "y", 2, 0, 0),
    ("s", "y", 2, 0, 1), ("s", "x", 0, 1),
    ("p", 3, 0), ("s", "y", 0, 1, 1), ("s", "y", 1, 1, 0), ("s", "y", 1, 1, 1), ("s", "y", 2, 1, 0),
    ("s", "y", 2, 1, 1),
    ("p", 3, 1), ("s", "x", 0, 3),
    ("p", 0, 1), ("s", "x", 0, 0), ("s", "x", 1, 2), ("s", "x", 1, 1), ("s", "x", 1, 3), ("s", "x", 1, 0),
    ("p", 1, 0), ("p", 0, 0),
    ("ua", 0, 0), ("ua", 0, 1), ("wm", 0, 2), ("pages", 0), ("pages", 1), ("wm", 0, 1), ("pages", 2),
    ("ua", 1, 0), ("ua", 1, 1), ("wm", 0, 3), ("pages", 3), ("ua", 2, 0), ("ua", 2, 1),
    ("wm", 1, 2), ("wm", 1, 1), ("uc", 0), ("wa", 0, 0), ("wa", 0, 1), ("wm", 1, 3), ("uc", 1), ("uc", 2),
    ("wa", 1, 0), ("uo", 0), ("wa", 1, 1), ("uo", 1), ("wo", 0), ("wo", 1), ("uo", 2),
)


def plus_slot(r):
    return 4 * Z_SET[r]


def minus_slot(r):
    return 4 * Z_SET[r] + 1


def x_slot(i):
    return 4 * X_SET[i // 2] + i % 2


def half_blocks(z, xl, c):
    def index(dz, other, flip):
        return lax.rem(z + dz + 8, 8) * 4 + (1 - xl if other else xl) * 2 + (1 - c if flip else c)

    found = []
    for flip in (0, 1):
        at = 2 * flip
        found += [(at, index(0, 0, flip), 0), (at + 1, index(0, 0, flip), 1)]
        for r in range(11):
            d = r // 3 + 1
            if r < 9:
                half, other = ((0, 0), (1, 0), (0, 1))[r % 3]
            else:
                half, other = (0, r - 9)
            found.append((plus_slot(r) + at, index(-d, other, flip), half))
            if r < 9:
                half, other = ((1, 0), (0, 0), (0, 1))[r % 3]
            else:
                half, other = (1, r - 9)
            found.append((minus_slot(r) + at, index(d, other, flip), half))
        for i, (dz, half) in enumerate(((0, 0), (0, 1), (1, 1), (-1, 1), (2, 1), (-2, 1), (3, 1), (-3, 1))):
            found.append((x_slot(i) + at, index(dz, 1, flip), half))
    return found


def kernel(order_hbm, owner_hbm, q_hbm, k_hbm, v_hbm, w_hbm, out_ref, pages_ref,
           order_ref, owner_ref, kv, q_raw, qx, top, acc, att, w, part, uy, ux, wx, wy, table_v, table_s, place, holder,
           load_sem, w_sem, z_ssem, z_rsem, x_ssem, x_rsem, d_ssem, d_rsem,
           uy_ssem, uy_rsem, ux_ssem, ux_rsem, wx_ssem, wx_rsem, wy_ssem, wy_rsem):
    grp, tp = lax.axis_index("grp"), lax.axis_index("tp")
    z, xl, c = grp // 4, lax.rem(grp // 2, 2), lax.rem(grp, 2)
    y, xh = tp // 2, lax.rem(tp, 2)

    def at_grp(z_to, xl_to, c_to):
        return (z_to * 4 + xl_to * 2 + c_to, tp)

    z_up = at_grp(lax.rem(z + 1, 8), xl, c)
    z_down = at_grp(lax.rem(z + 7, 8), xl, c)
    x_near = at_grp(z, 1 - xl, c)
    core = at_grp(z, xl, 1 - c)
    y_up = (grp, lax.rem(y + 1, 4) * 2 + xh)
    y_down = (grp, lax.rem(y + 3, 4) * 2 + xh)
    x_far = (grp, y * 2 + 1 - xh)

    barrier = pltpu.get_barrier_semaphore()
    for near in (z_up, z_down, x_near, core, y_up, y_down, x_far):
        pl.semaphore_signal(barrier, inc=1, device_id=near, device_id_type=MESH)

    loads = []
    for half in range(2):
        for ref, lane in ((k_hbm, 0), (v_hbm, HEAD)):
            loads.append(pltpu.make_async_copy(
                ref.at[pl.ds(8 * half, 8)], kv.at[pl.ds(8 * half, 8), :, pl.ds(lane, HEAD)],
                load_sem.at[len(loads)]))
    load_q = pltpu.make_async_copy(q_hbm, q_raw, load_sem.at[4])
    load_w = pltpu.make_async_copy(w_hbm, w, w_sem)
    for load in loads:
        load.start()
    load_order = pltpu.make_async_copy(order_hbm, order_ref, load_sem.at[6])
    load_owner = pltpu.make_async_copy(owner_hbm, owner_ref, load_sem.at[7])
    load_order.start()
    load_owner.start()
    load_q.start()
    load_w.start()

    for slot, block, half in half_blocks(z, xl, c):
        place[2 * block + half] = slot + 0 * grp
        holder[slot] = block

    for load in loads:
        load.wait()
    pl.semaphore_wait(barrier, 7)

    sent = []

    def remote(src, dst, ssem, rsem, to):
        return pltpu.make_async_remote_copy(src_ref=src, dst_ref=dst, send_sem=ssem, recv_sem=rsem,
                                            device_id=to, device_id_type=MESH)

    def slots(first, count=1):
        return kv.at[pl.ds(8 * first, 8 * count)]

    def plus(r, src):
        return remote(slots(src), slots(plus_slot(r)), z_ssem.at[0, r], z_rsem.at[0, r], z_up)

    def minus(r, src):
        return remote(slots(src), slots(minus_slot(r)), z_ssem.at[1, r], z_rsem.at[1, r], z_down)

    def cross(i, src):
        return remote(slots(src), slots(x_slot(i)), x_ssem.at[i], x_rsem.at[i], x_near)

    def twin(k):
        return remote(slots(4 * k, 2), slots(4 * k + 2, 2), d_ssem.at[k], d_rsem.at[k], core)

    def begin(make, *which):
        make(*which).start()
        sent.append((make, which))

    begin(cross, 0, 0)
    begin(plus, 0, 0)
    begin(minus, 0, 1)
    begin(twin, 0)
    begin(cross, 1, 1)
    begin(plus, 1, 1)
    begin(minus, 1, 0)

    def z_step(r):
        plus(r, 0).wait_recv()
        minus(r, 0).wait_recv()
        if r <= 6:
            begin(plus, r + 3, plus_slot(r))
            begin(minus, r + 3, minus_slot(r))
        if r == 8:
            begin(plus, 10, plus_slot(8))
        if r % 3 == 0 and r <= 6:
            begin(cross, 2 + 2 * (r // 3), minus_slot(r))
        if r % 3 == 1 and r <= 7:
            begin(cross, 3 + 2 * (r // 3), plus_slot(r))
        begin(twin, Z_SET[r])

    def x_step(i):
        cross(i, 0).wait_recv()
        if i == 0:
            begin(plus, 2, x_slot(0))
            begin(minus, 2, x_slot(0))
        if i == 6:
            begin(minus, 10, x_slot(6))
        if i % 2 == 1:
            begin(twin, X_SET[i // 2])

    before = {
        1: (("x", 0), ("z", 0), ("x", 1), ("z", 1)),
        3: (("z", 2), ("x", 2)),
        4: (("z", 3), ("x", 3)),
        5: (("z", 4),),
        6: (("z", 5),),
        7: (("z", 6), ("x", 4)),
        8: (("x", 5), ("z", 7)),
        10: (("z", 8), ("x", 6)),
        11: (("z", 9),),
        12: (("x", 7),),
        13: (("z", 10),),
    }

    def softmax_step(k, first):
        block = kv[pl.ds(32 * k, 32)].reshape(512, 2 * HEAD)
        rows = []
        for j in range(4):
            seen = order_ref[holder[4 * k + j]] < here
            if first and j < 2:
                seen = True
            rows.append(jnp.full((HEAD, HEAD), jnp.where(seen, 0.0, NEG), jnp.float32).astype(jnp.bfloat16))
        keys = jnp.concatenate([block[:, :HEAD], jnp.concatenate(rows, axis=0)], axis=1)
        values = jnp.concatenate([block[:, HEAD:], jnp.ones((512, HEAD), jnp.bfloat16)], axis=1)
        scores = [lax.dot_general(qx[h], keys, (((1,), (1,)), ((), ())), preferred_element_type=jnp.float32)
                  for h in range(QPK)]
        for h in range(QPK):
            tiles = [scores[h][:, HEAD * j:HEAD * (j + 1)] for j in range(4)]
            if first:
                row = lax.broadcasted_iota(jnp.int32, (ROWS, HEAD), 0)
                lane = lax.broadcasted_iota(jnp.int32, (ROWS, HEAD), 1)
                for j in range(2):
                    tiles[j] = jnp.where(lane + HEAD * j <= row, tiles[j], NEG)
            peak = jnp.max(jnp.maximum(jnp.maximum(tiles[0], tiles[1]), jnp.maximum(tiles[2], tiles[3])),
                           axis=1, keepdims=True)
            if first:
                new = jnp.broadcast_to(peak, (ROWS, HEAD))
            else:
                old = top[h]
                new = jnp.maximum(old, peak)
            expo = [jnp.exp2((tile - new) * SCALE2).astype(jnp.bfloat16) for tile in tiles]
            gained = jnp.dot(jnp.concatenate(expo, axis=1), values, preferred_element_type=jnp.float32)
            top[h] = new
            if first:
                acc[h] = gained
            else:
                factor = jnp.exp2((old - new) * SCALE2)
                acc[h] = acc[h] * jnp.concatenate([factor, factor], axis=1) + gained

    load_order.wait()
    load_owner.wait()
    here = order_ref[grp]
    load_q.wait()
    lane = lax.broadcasted_iota(jnp.int32, (ROWS, HEAD), 1)
    unit = jnp.where(lane == 0, 1.0, 0.0).astype(jnp.bfloat16)
    for h in range(QPK):
        qx[h] = jnp.concatenate([q_raw[:, HEAD * h:HEAD * (h + 1)], unit], axis=1)
    twin(0).wait_recv()
    softmax_step(0, True)

    @pl.loop(1, N_SET)
    def _(k):
        for at, events in before.items():
            @pl.when(k == at)
            def _():
                for kind, r in events:
                    (z_step if kind == "z" else x_step)(r)
        twin(k).wait_recv()
        softmax_step(k, False)

    for h in range(QPK):
        att[:, HEAD * h:HEAD * (h + 1)] = (acc[h, :, :HEAD] / acc[h, :, HEAD:]).astype(jnp.bfloat16)
    load_w.wait()

    def project(i, j):
        first = (lax.rem(y + i, 4) * 2 + (1 - xh if j else xh)) * COLS

        for n in range(2):
            at = pl.multiple_of(first + n * 512, 512)
            part[i, j, :, pl.ds(n * 512, 512)] = jnp.dot(
                att[...], w[:, pl.ds(at, 512)], preferred_element_type=jnp.float32).astype(jnp.bfloat16)

    def u_rows(g):
        return pl.ds(sum(Y_ROWS[:g]), Y_ROWS[g])

    def w_rows(g):
        return pl.ds(sum(Y_ROWS) + sum(X_ROWS[:g]), X_ROWS[g])

    def u_near(g, way, n):
        i, j = ((2, 0), (1, 1), (1, 0))[n] if way == 0 else ((2, 1), (3, 0), (3, 1))[n]
        return remote(part.at[i, j, u_rows(g)], uy.at[g, way, n, pl.ds(0, Y_ROWS[g])],
                      uy_ssem.at[g, way, n], uy_rsem.at[g, way, n], (y_up, y_down)[way])

    def u_far(g):
        return remote(part.at[0, 1, u_rows(g)], ux.at[g, pl.ds(0, Y_ROWS[g])], ux_ssem.at[g], ux_rsem.at[g], x_far)

    def w_far(g, i):
        return remote(part.at[i, 1, w_rows(g)], wx.at[g, i, pl.ds(0, X_ROWS[g])],
                      wx_ssem.at[g, i], wx_rsem.at[g, i], x_far)

    def w_near(g, way, n):
        i = (2, 1, 1)[n] if way == 0 else (2, 3, 3)[n]
        left = (0, 1, 0)[n] if way == 0 else (1, 0, 1)[n]
        return remote(part.at[i, 0, w_rows(g), pl.ds(512 * left, 512)], wy.at[g, way, n, pl.ds(0, X_ROWS[g])],
                      wy_ssem.at[g, way, n], wy_rsem.at[g, way, n], (y_up, y_down)[way])

    def wide(a):
        return a.astype(jnp.float32)

    def u_add(g, way):
        i, j = ((1, 0), (3, 1))[way]
        u_near(g, way, 0).wait_recv()
        came = uy[g, way, 0, :Y_ROWS[g]]
        part[i, j, u_rows(g)] = (wide(part[i, j, u_rows(g)]) + wide(came)).astype(jnp.bfloat16)
        begin(u_near, g, way, 2)

    def u_total(g, j):
        size = Y_ROWS[g]
        return wide(part[0, j, u_rows(g)]) + wide(uy[g, 0, 2 - j, :size]) + wide(uy[g, 1, 1 + j, :size])

    def u_cross(g):
        for way in (0, 1):
            for n in (1, 2):
                u_near(g, way, n).wait_recv()
        part[0, 1, u_rows(g)] = u_total(g, 1).astype(jnp.bfloat16)
        begin(u_far, g)

    def u_out(g):
        u_far(g).wait_recv()
        out_ref[u_rows(g)] = (u_total(g, 0) + wide(ux[g, :Y_ROWS[g]])).astype(jnp.bfloat16)

    def w_mid(g, i):
        at = w_rows(g)
        w_far(g, i).wait_recv()
        part[i, 0, at] = (wide(part[i, 0, at]) + wide(wx[g, i, :X_ROWS[g]])).astype(jnp.bfloat16)
        if i == 2:
            begin(w_near, g, 0, 0)
            begin(w_near, g, 1, 0)
        else:
            begin(w_near, g, (1 if i == 3 else 0), 1)

    def w_add(g, way):
        at, cols = w_rows(g), pl.ds(512 * way, 512)
        i = (1, 3)[way]
        w_near(g, way, 0).wait_recv()
        came = wy[g, way, 0, :X_ROWS[g]]
        part[i, 0, at, cols] = (wide(part[i, 0, at, cols]) + wide(came)).astype(jnp.bfloat16)
        begin(w_near, g, way, 2)

    def w_out(g):
        at, size = w_rows(g), X_ROWS[g]
        w_far(g, 0).wait_recv()
        for way in (0, 1):
            for n in (1, 2):
                w_near(g, way, n).wait_recv()
        total = wide(part[0, 0, at]) + wide(wx[g, 0, :size])
        came = [wide(wy[g, 0, 2 - left, :size]) + wide(wy[g, 1, 1 + left, :size]) for left in (0, 1)]
        out_ref[at] = (total + jnp.concatenate(came, axis=1)).astype(jnp.bfloat16)

    def find_pages():
        lanes = lax.broadcasted_iota(jnp.int32, (8, 128), 1)

        def look(i, carry):
            found, count = carry
            mine = owner_ref[i] == grp
            found = jnp.where((lanes == count) & mine, i, found)
            return found, count + jnp.where(mine, 1, 0)

        found, count = lax.fori_loop(0, NPAGES, look, (jnp.zeros((8, 128), jnp.int32), 0 * grp), unroll=8)
        table_v[...] = found
        fetch = pltpu.make_async_copy(table_v, table_s, load_sem.at[5])
        fetch.start()
        fetch.wait()
        return count

    def hand_pages(first, count):
        @pl.loop(first, first + SLOTS // 4)
        def _(s):
            page = table_s[0, s]
            slot = place[page // 8]
            rows = kv[slot * 8 + lax.rem(page, 8)]
            pages_ref[s] = jnp.where(s < count, rows, jnp.zeros_like(rows))

    owned = 0
    for step, *which in ORDER:
        if step == "p":
            project(*which)
        elif step == "s":
            begin(u_near if which[0] == "y" else w_far, *which[1:])
        elif step == "pages":
            if which[0] == 0:
                owned = find_pages()
            hand_pages(which[0] * (SLOTS // 4), owned)
        else:
            {"ua": u_add, "uc": u_cross, "uo": u_out, "wm": w_mid, "wa": w_add, "wo": w_out}[step](*which)

    for make, which in sent:
        make(*which).wait_send()


def on_device(queries, key_rows, value_rows, out_weight, block_order, page_owner):
    dma = pltpu.SemaphoreType.DMA
    vmem = pltpu.VMEM
    bf16, f32, i32 = jnp.bfloat16, jnp.float32, jnp.int32
    hbm = pl.BlockSpec(memory_space=pltpu.HBM)
    vmem_out = pl.BlockSpec(memory_space=pltpu.VMEM)
    made = pl.pallas_call(
        kernel,
        name="attend",
        out_shape=(vmem((ROWS, COLS), bf16), vmem((SLOTS, PAGE, 2 * HEAD), bf16)),
        in_specs=[hbm] * 6,
        out_specs=(vmem_out, vmem_out),
        scratch_shapes=[
            pltpu.SMEM((32,), i32),
            pltpu.SMEM((NPAGES,), i32),
            vmem((NPAGES, PAGE, 2 * HEAD), bf16),
            vmem((ROWS, QPK * HEAD), bf16),
            vmem((QPK, ROWS, 2 * HEAD), bf16),
            vmem((QPK, ROWS, HEAD), f32),
            vmem((QPK, ROWS, 2 * HEAD), f32),
            vmem((ROWS, QPK * HEAD), bf16),
            vmem((QPK * HEAD, 8 * COLS), bf16),
            vmem((4, 2, ROWS, COLS), bf16),
            vmem((Y_FIRST, 2, 3, max(Y_ROWS), COLS), bf16),
            vmem((Y_FIRST, max(Y_ROWS), COLS), bf16),
            vmem((X_FIRST, 4, max(X_ROWS), COLS), bf16),
            vmem((X_FIRST, 2, 3, max(X_ROWS), COLS // 2), bf16),
            vmem((8, 128), i32),
            pltpu.SMEM((8, 128), i32),
            pltpu.SMEM((64,), i32),
            pltpu.SMEM((64,), i32),
            dma((8,)), dma,
            dma((2, 11)), dma((2, 11)), dma((8,)), dma((8,)), dma((N_SET,)), dma((N_SET,)),
            dma((Y_FIRST, 2, 3)), dma((Y_FIRST, 2, 3)), dma((Y_FIRST,)), dma((Y_FIRST,)),
            dma((X_FIRST, 4)), dma((X_FIRST, 4)), dma((X_FIRST, 2, 3)), dma((X_FIRST, 2, 3)),
        ],
        compiler_params=pltpu.CompilerParams(
            collective_id=0, has_side_effects=True, vmem_limit_bytes=56 * 2**20),
    )(block_order, page_owner.reshape(NPAGES), queries,
      key_rows.reshape(PAGE, PAGE, HEAD), value_rows.reshape(PAGE, PAGE, HEAD), out_weight)
    return made


def solution(mesh):
    placed = (P("grp", "tp"), P("grp", "tp"), P("grp", "tp"), P("tp", None), P(), P())
    return jax.shard_map(
        on_device,
        mesh=mesh,
        in_specs=placed,
        out_specs=(P("grp", "tp"), P("grp", None, "tp")),
        check_vma=False,
    )
```

```python
import functools

import jax
import jax.numpy as jnp
from jax import lax
from jax.experimental import pallas as pl
from jax.experimental.pallas import tpu as pltpu
from jax.sharding import PartitionSpec as P

MESH = pl.DeviceIdType.MESH
HEAD = 128
QPK = 4
ROWS = 256
PAGE = 16
COLS = 1024
SLOTS = 64
NPAGES = 512
NEG = -1e30
SCALE2 = 128.0 ** -0.5 * 1.4426950408889634

Z_SET = (1, 3, 4, 5, 7, 8, 9, 10, 12, 13, 15)
X_SET = (2, 6, 11, 14)
N_SET = 16

Y_ROWS = (64, 64, 32)
X_ROWS = (48, 48)
Y_FIRST, X_FIRST = len(Y_ROWS), len(X_ROWS)
NEAR = sum(Y_ROWS)
ORDER = (
    ("p", 2, 1), ("sn", 0, 0, 0), ("sn", 0, 1, 0), ("sx", 0, 2), ("p", 1, 1), ("sn", 0, 0, 1),
    ("sa", 0), ("sn", 1, 0, 0), ("sn", 1, 0, 1), ("sn", 2, 0, 0), ("sn", 2, 0, 1), ("sx", 0, 1), ("p", 3, 1),
    ("sn", 0, 1, 1), ("sa", 1), ("sn", 1, 1, 0), ("sn", 1, 1, 1), ("sn", 2, 1, 0), ("sn", 2, 1, 1), ("sa", 2),
    ("sx", 0, 3), ("p", 0, 1), ("sx", 0, 0), ("sx", 1, 2), ("sx", 1, 1), ("sx", 1, 3), ("sx", 1, 0),
    ("p", 2, 0), ("p", 1, 0), ("p", 3, 0), ("p", 0, 0), ("forward",), ("pages", 0), ("pages", 1), ("wm", 0, 2),
    ("na", 0, 0), ("na", 0, 1), ("pages", 2), ("pages", 3), ("wm", 0, 1), ("sum", 0), ("wm", 0, 3),
    ("na", 1, 0), ("na", 1, 1), ("sum", 1), ("sum", 2), ("sum", 3), ("wm", 1, 2), ("na", 2, 0), ("na", 2, 1),
    ("wa", 0, 0), ("wa", 0, 1), ("wm", 1, 1), ("nc", 0), ("wm", 1, 3), ("nc", 1), ("wa", 1, 0), ("wa", 1, 1),
    ("nc", 2), ("wo", 0), ("no", 0), ("wo", 1), ("no", 1), ("no", 2),
)


def plus_slot(r):
    return 4 * Z_SET[r]


def minus_slot(r):
    return 4 * Z_SET[r] + 1


def x_slot(i):
    return 4 * X_SET[i // 2] + i % 2


def half_blocks(z, xl, c):
    def index(dz, other, flip):
        return lax.rem(z + dz + 8, 8) * 4 + (1 - xl if other else xl) * 2 + (1 - c if flip else c)

    found = []
    for flip in (0, 1):
        at = 2 * flip
        found += [(at, index(0, 0, flip), 0), (at + 1, index(0, 0, flip), 1)]
        for r in range(11):
            d = r // 3 + 1
            if r < 9:
                half, other = ((0, 0), (1, 0), (0, 1))[r % 3]
            else:
                half, other = (0, r - 9)
            found.append((plus_slot(r) + at, index(-d, other, flip), half))
            if r < 9:
                half, other = ((1, 0), (0, 0), (0, 1))[r % 3]
            else:
                half, other = (1, r - 9)
            found.append((minus_slot(r) + at, index(d, other, flip), half))
        for i, (dz, half) in enumerate(((0, 0), (0, 1), (1, 1), (-1, 1), (2, 1), (-2, 1), (3, 1), (-3, 1))):
            found.append((x_slot(i) + at, index(dz, 1, flip), half))
    return found


def kernel(order_hbm, owner_hbm, q_hbm, k_hbm, v_hbm, w_hbm, out_ref, pages_ref,
           slices, gathered, own, order_ref, owner_ref, kv, q_raw, qx, top, acc, att, w, part, uy, ux, wx, wy, table_v, table_s, place, holder,
           load_sem, w_sem, z_ssem, z_rsem, x_ssem, x_rsem, d_ssem, d_rsem,
           slice_ssem, slice_rsem, half_ssem, half_rsem, att_ssem, att_rsem,
           uy_ssem, uy_rsem, ux_ssem, ux_rsem, wx_ssem, wx_rsem, wy_ssem, wy_rsem):
    grp, tp = lax.axis_index("grp"), lax.axis_index("tp")
    z, xl, c = grp // 4, lax.rem(grp // 2, 2), lax.rem(grp, 2)
    y, xh = tp // 2, lax.rem(tp, 2)

    def at_grp(z_to, xl_to, c_to):
        return (z_to * 4 + xl_to * 2 + c_to, tp)

    z_up = at_grp(lax.rem(z + 1, 8), xl, c)
    z_down = at_grp(lax.rem(z + 7, 8), xl, c)
    x_near = at_grp(z, 1 - xl, c)
    core = at_grp(z, xl, 1 - c)
    y_up = (grp, lax.rem(y + 1, 4) * 2 + xh)
    y_down = (grp, lax.rem(y + 3, 4) * 2 + xh)
    y_far = (grp, lax.rem(y + 2, 4) * 2 + xh)
    x_far = (grp, y * 2 + 1 - xh)

    barrier = pltpu.get_barrier_semaphore()
    for near in (z_up, z_down, x_near, core, y_up, y_down, y_far, x_far):
        pl.semaphore_signal(barrier, inc=1, device_id=near, device_id_type=MESH)

    loads = []
    for half in range(2):
        for ref, lane in ((k_hbm, 0), (v_hbm, HEAD)):
            loads.append(pltpu.make_async_copy(
                ref.at[pl.ds(8 * half, 8)], kv.at[pl.ds(8 * half, 8), :, pl.ds(lane, HEAD)],
                load_sem.at[len(loads)]))
    load_q = pltpu.make_async_copy(q_hbm, q_raw, load_sem.at[4])
    load_w = pltpu.make_async_copy(w_hbm, w, w_sem)
    for load in loads:
        load.start()
    load_order = pltpu.make_async_copy(order_hbm, order_ref, load_sem.at[6])
    load_owner = pltpu.make_async_copy(owner_hbm, owner_ref, load_sem.at[7])
    load_order.start()
    load_owner.start()
    load_q.start()
    load_w.start()

    for slot, block, half in half_blocks(z, xl, c):
        place[2 * block + half] = slot + 0 * grp
        holder[slot] = block

    for load in loads:
        load.wait()
    pl.semaphore_wait(barrier, 8)

    sent = []

    def remote(src, dst, ssem, rsem, to):
        return pltpu.make_async_remote_copy(src_ref=src, dst_ref=dst, send_sem=ssem, recv_sem=rsem,
                                            device_id=to, device_id_type=MESH)

    def slots(first, count=1):
        return kv.at[pl.ds(8 * first, 8 * count)]

    def plus(r, src):
        return remote(slots(src), slots(plus_slot(r)), z_ssem.at[0, r], z_rsem.at[0, r], z_up)

    def minus(r, src):
        return remote(slots(src), slots(minus_slot(r)), z_ssem.at[1, r], z_rsem.at[1, r], z_down)

    def cross(i, src):
        return remote(slots(src), slots(x_slot(i)), x_ssem.at[i], x_rsem.at[i], x_near)

    def twin(k):
        return remote(slots(4 * k, 2), slots(4 * k + 2, 2), d_ssem.at[k], d_rsem.at[k], core)

    def begin(make, *which):
        make(*which).start()
        sent.append((make, which))

    begin(cross, 0, 0)
    begin(plus, 0, 0)
    begin(minus, 0, 1)
    begin(twin, 0)
    begin(cross, 1, 1)
    begin(plus, 1, 1)
    begin(minus, 1, 0)

    ahead = (y_up, y_down, y_far)
    steps = (1, 3, 2)

    def weight_slice(n):
        first = (lax.rem(y + steps[n], 4) * 2 + xh) * COLS
        src = w_hbm.at[pl.ds(pl.multiple_of(256 * c, 256), 256), pl.ds(pl.multiple_of(first, COLS), COLS)]
        return remote(src, slices.at[n, pl.ds(pl.multiple_of(256 * c, 256), 256)],
                      slice_ssem.at[n], slice_rsem.at[n], ahead[n])

    def weight_half(n):
        half = slices.at[n, pl.ds(pl.multiple_of(256 * c, 256), 256)]
        return remote(half, half, half_ssem.at[n], half_rsem.at[n], core)

    for n in range(3):
        begin(weight_slice, n)

    def z_step(r):
        plus(r, 0).wait_recv()
        minus(r, 0).wait_recv()
        if r <= 6:
            begin(plus, r + 3, plus_slot(r))
            begin(minus, r + 3, minus_slot(r))
        if r == 8:
            begin(plus, 10, plus_slot(8))
        if r % 3 == 0 and r <= 6:
            begin(cross, 2 + 2 * (r // 3), minus_slot(r))
        if r % 3 == 1 and r <= 7:
            begin(cross, 3 + 2 * (r // 3), plus_slot(r))
        begin(twin, Z_SET[r])

    def x_step(i):
        cross(i, 0).wait_recv()
        if i == 0:
            begin(plus, 2, x_slot(0))
            begin(minus, 2, x_slot(0))
        if i == 6:
            begin(minus, 10, x_slot(6))
        if i % 2 == 1:
            begin(twin, X_SET[i // 2])

    before = {
        1: (("x", 0), ("z", 0), ("x", 1), ("z", 1)),
        3: (("z", 2), ("x", 2)),
        4: (("z", 3), ("x", 3)),
        5: (("z", 4),),
        6: (("z", 5),),
        7: (("z", 6), ("x", 4)),
        8: (("x", 5), ("z", 7)),
        10: (("z", 8), ("x", 6)),
        11: (("z", 9),),
        12: (("x", 7),),
        13: (("z", 10),),
    }

    def softmax_step(k, first):
        block = kv[pl.ds(32 * k, 32)].reshape(512, 2 * HEAD)
        rows = []
        for j in range(4):
            seen = order_ref[holder[4 * k + j]] < here
            if first and j < 2:
                seen = True
            rows.append(jnp.full((HEAD, HEAD), jnp.where(seen, 0.0, NEG), jnp.float32).astype(jnp.bfloat16))
        keys = jnp.concatenate([block[:, :HEAD], jnp.concatenate(rows, axis=0)], axis=1)
        values = jnp.concatenate([block[:, HEAD:], jnp.ones((512, HEAD), jnp.bfloat16)], axis=1)
        scores = [lax.dot_general(qx[h], keys, (((1,), (1,)), ((), ())), preferred_element_type=jnp.float32)
                  for h in range(QPK)]
        for h in range(QPK):
            tiles = [scores[h][:, HEAD * j:HEAD * (j + 1)] for j in range(4)]
            if first:
                row = lax.broadcasted_iota(jnp.int32, (ROWS, HEAD), 0)
                lane = lax.broadcasted_iota(jnp.int32, (ROWS, HEAD), 1)
                for j in range(2):
                    tiles[j] = jnp.where(lane + HEAD * j <= row, tiles[j], NEG)
            peak = jnp.max(jnp.maximum(jnp.maximum(tiles[0], tiles[1]), jnp.maximum(tiles[2], tiles[3])),
                           axis=1, keepdims=True)
            if first:
                new = jnp.broadcast_to(peak, (ROWS, HEAD))
            else:
                old = top[h]
                new = jnp.maximum(old, peak)
            expo = [jnp.exp2((tile - new) * SCALE2).astype(jnp.bfloat16) for tile in tiles]
            gained = jnp.dot(jnp.concatenate(expo, axis=1), values, preferred_element_type=jnp.float32)
            top[h] = new
            if first:
                acc[h] = gained
            else:
                factor = jnp.exp2((old - new) * SCALE2)
                acc[h] = acc[h] * jnp.concatenate([factor, factor], axis=1) + gained

    load_order.wait()
    load_owner.wait()
    here = order_ref[grp]
    load_q.wait()
    lane = lax.broadcasted_iota(jnp.int32, (ROWS, HEAD), 1)
    unit = jnp.where(lane == 0, 1.0, 0.0).astype(jnp.bfloat16)
    for h in range(QPK):
        qx[h] = jnp.concatenate([q_raw[:, HEAD * h:HEAD * (h + 1)], unit], axis=1)
    twin(0).wait_recv()
    softmax_step(0, True)

    @pl.loop(1, N_SET)
    def _(k):
        for at, events in before.items():
            @pl.when(k == at)
            def _():
                for kind, r in events:
                    (z_step if kind == "z" else x_step)(r)
        twin(k).wait_recv()
        softmax_step(k, False)

    for h in range(QPK):
        att[:, HEAD * h:HEAD * (h + 1)] = (acc[h, :, :HEAD] / acc[h, :, HEAD:]).astype(jnp.bfloat16)
    load_w.wait()

    def cols_of(i, j):
        return (lax.rem(y + i, 4) * 2 + (1 - xh if j else xh)) * COLS

    def project(i, j):
        rows = pl.ds(0, ROWS) if j else pl.ds(NEAR, ROWS - NEAR)
        for n in range(2):
            at = pl.multiple_of(cols_of(i, j) + n * 512, 512)
            part[i, j, rows, pl.ds(n * 512, 512)] = jnp.dot(
                att[rows], w[:, pl.ds(at, 512)], preferred_element_type=jnp.float32).astype(jnp.bfloat16)

    def u_rows(g):
        return pl.ds(sum(Y_ROWS[:g]), Y_ROWS[g])

    def w_rows(g):
        return pl.ds(NEAR + sum(X_ROWS[:g]), X_ROWS[g])

    def att_rows(n):
        return remote(att.at[pl.ds(0, NEAR)], gathered.at[n], att_ssem.at[n], att_rsem.at[n], ahead[n])

    def along_y(way, n, j, rows, to, ssem, rsem):
        i = (2, 1, 1)[n] if way == 0 else (2, 3, 3)[n]
        left = (0, 1, 0)[n] if way == 0 else (1, 0, 1)[n]
        return remote(part.at[i, j, rows, pl.ds(512 * left, 512)], to, ssem, rsem, (y_up, y_down)[way])

    def u_near(g, way, n):
        return along_y(way, n, 1, u_rows(g), uy.at[g, way, n, pl.ds(0, Y_ROWS[g])],
                       uy_ssem.at[g, way, n], uy_rsem.at[g, way, n])

    def w_near(g, way, n):
        return along_y(way, n, 0, w_rows(g), wy.at[g, way, n, pl.ds(0, X_ROWS[g])],
                       wy_ssem.at[g, way, n], wy_rsem.at[g, way, n])

    def u_far(g):
        return remote(part.at[0, 1, u_rows(g)], ux.at[g, pl.ds(0, Y_ROWS[g])], ux_ssem.at[g], ux_rsem.at[g], x_far)

    def w_far(g, i):
        return remote(part.at[i, 1, w_rows(g)], wx.at[g, i, pl.ds(0, X_ROWS[g])],
                      wx_ssem.at[g, i], wx_rsem.at[g, i], x_far)

    def wide(a):
        return a.astype(jnp.float32)

    def add_half(near, j, rows, came, g, way):
        i, cols = (1, 3)[way], pl.ds(512 * way, 512)
        near(g, way, 0).wait_recv()
        part[i, j, rows, cols] = (wide(part[i, j, rows, cols]) + wide(came())).astype(jnp.bfloat16)
        begin(near, g, way, 2)

    def both_ways(near, g):
        for way in (0, 1):
            for n in (1, 2):
                near(g, way, n).wait_recv()

    def came_along_y(buf, g, size):
        return jnp.concatenate([wide(buf[g, 0, 2 - left, :size]) + wide(buf[g, 1, 1 + left, :size])
                                for left in (0, 1)], axis=1)

    def u_add(g, way):
        add_half(u_near, 1, u_rows(g), lambda: uy[g, way, 0, :Y_ROWS[g]], g, way)

    def u_cross(g):
        both_ways(u_near, g)
        part[0, 1, u_rows(g)] = (wide(part[0, 1, u_rows(g)]) + came_along_y(uy, g, Y_ROWS[g])).astype(jnp.bfloat16)
        begin(u_far, g)

    def u_out(g):
        u_far(g).wait_recv()
        out_ref[u_rows(g)] = (own[u_rows(g)] + wide(ux[g, :Y_ROWS[g]])).astype(jnp.bfloat16)

    def forward():
        for n in range(3):
            weight_slice(n).wait_recv()
            begin(weight_half, n)

    def own_sum(n):
        if n == 0:
            at = pl.multiple_of(cols_of(0, 0), COLS)
            own[...] = jnp.dot(att[pl.ds(0, NEAR)], w[:, pl.ds(at, COLS)], preferred_element_type=jnp.float32)
        else:
            att_rows(n - 1).wait_recv()
            weight_half(n - 1).wait_recv()
            own[...] += jnp.dot(gathered[n - 1], slices[n - 1], preferred_element_type=jnp.float32)

    def w_mid(g, i):
        at = w_rows(g)
        w_far(g, i).wait_recv()
        part[i, 0, at] = (wide(part[i, 0, at]) + wide(wx[g, i, :X_ROWS[g]])).astype(jnp.bfloat16)
        if i == 2:
            begin(w_near, g, 0, 0)
            begin(w_near, g, 1, 0)
        else:
            begin(w_near, g, (1 if i == 3 else 0), 1)

    def w_add(g, way):
        add_half(w_near, 0, w_rows(g), lambda: wy[g, way, 0, :X_ROWS[g]], g, way)

    def w_out(g):
        at, size = w_rows(g), X_ROWS[g]
        w_far(g, 0).wait_recv()
        both_ways(w_near, g)
        total = wide(part[0, 0, at]) + wide(wx[g, 0, :size]) + came_along_y(wy, g, size)
        out_ref[at] = total.astype(jnp.bfloat16)

    def find_pages():
        lanes = lax.broadcasted_iota(jnp.int32, (8, 128), 1)

        def look(i, carry):
            found, count = carry
            mine = owner_ref[i] == grp
            found = jnp.where((lanes == count) & mine, i, found)
            return found, count + jnp.where(mine, 1, 0)

        found, count = lax.fori_loop(0, NPAGES, look, (jnp.zeros((8, 128), jnp.int32), 0 * grp), unroll=8)
        table_v[...] = found
        fetch = pltpu.make_async_copy(table_v, table_s, load_sem.at[5])
        fetch.start()
        fetch.wait()
        return count

    def hand_pages(first, count):
        @pl.loop(first, first + SLOTS // 4)
        def _(s):
            page = table_s[0, s]
            slot = place[page // 8]
            rows = kv[slot * 8 + lax.rem(page, 8)]
            pages_ref[s] = jnp.where(s < count, rows, jnp.zeros_like(rows))

    owned = 0
    for step, *which in ORDER:
        if step == "p":
            project(*which)
        elif step in ("sa", "sn", "sx"):
            begin({"sa": att_rows, "sn": u_near, "sx": w_far}[step], *which)
        elif step == "pages":
            if which[0] == 0:
                owned = find_pages()
            hand_pages(which[0] * (SLOTS // 4), owned)
        else:
            {"na": u_add, "nc": u_cross, "no": u_out, "wm": w_mid, "wa": w_add, "wo": w_out,
             "forward": forward, "sum": own_sum}[step](*which)

    for make, which in sent:
        make(*which).wait_send()


def on_device(queries, key_rows, value_rows, out_weight, block_order, page_owner):
    dma = pltpu.SemaphoreType.DMA
    vmem = pltpu.VMEM
    bf16, f32, i32 = jnp.bfloat16, jnp.float32, jnp.int32
    hbm = pl.BlockSpec(memory_space=pltpu.HBM)
    vmem_out = pl.BlockSpec(memory_space=pltpu.VMEM)
    made = pl.pallas_call(
        kernel,
        name="attend",
        out_shape=(vmem((ROWS, COLS), bf16), vmem((SLOTS, PAGE, 2 * HEAD), bf16)),
        in_specs=[hbm] * 6,
        out_specs=(vmem_out, vmem_out),
        scratch_shapes=[
            vmem((3, QPK * HEAD, COLS), bf16),
            vmem((3, NEAR, QPK * HEAD), bf16),
            vmem((NEAR, COLS), f32),
            pltpu.SMEM((32,), i32),
            pltpu.SMEM((NPAGES,), i32),
            vmem((NPAGES, PAGE, 2 * HEAD), bf16),
            vmem((ROWS, QPK * HEAD), bf16),
            vmem((QPK, ROWS, 2 * HEAD), bf16),
            vmem((QPK, ROWS, HEAD), f32),
            vmem((QPK, ROWS, 2 * HEAD), f32),
            vmem((ROWS, QPK * HEAD), bf16),
            vmem((QPK * HEAD, 8 * COLS), bf16),
            vmem((4, 2, ROWS, COLS), bf16),
            vmem((Y_FIRST, 2, 3, max(Y_ROWS), COLS // 2), bf16),
            vmem((Y_FIRST, max(Y_ROWS), COLS), bf16),
            vmem((X_FIRST, 4, max(X_ROWS), COLS), bf16),
            vmem((X_FIRST, 2, 3, max(X_ROWS), COLS // 2), bf16),
            vmem((8, 128), i32),
            pltpu.SMEM((8, 128), i32),
            pltpu.SMEM((64,), i32),
            pltpu.SMEM((64,), i32),
            dma((8,)), dma,
            dma((2, 11)), dma((2, 11)), dma((8,)), dma((8,)), dma((N_SET,)), dma((N_SET,)),
            dma((3,)), dma((3,)), dma((3,)), dma((3,)), dma((3,)), dma((3,)),
            dma((Y_FIRST, 2, 3)), dma((Y_FIRST, 2, 3)), dma((Y_FIRST,)), dma((Y_FIRST,)),
            dma((X_FIRST, 4)), dma((X_FIRST, 4)), dma((X_FIRST, 2, 3)), dma((X_FIRST, 2, 3)),
        ],
        compiler_params=pltpu.CompilerParams(
            collective_id=0, has_side_effects=True, vmem_limit_bytes=56 * 2**20),
    )(block_order, page_owner.reshape(NPAGES), queries,
      key_rows.reshape(PAGE, PAGE, HEAD), value_rows.reshape(PAGE, PAGE, HEAD), out_weight)
    return made


def solution(mesh):
    placed = (P("grp", "tp"), P("grp", "tp"), P("grp", "tp"), P("tp", None), P(), P())
    return jax.shard_map(
        on_device,
        mesh=mesh,
        in_specs=placed,
        out_specs=(P("grp", "tp"), P("grp", None, "tp")),
        check_vma=False,
    )
```

```python
import functools

import jax
import jax.numpy as jnp
from jax import lax
from jax.experimental import pallas as pl
from jax.experimental.pallas import tpu as pltpu
from jax.sharding import PartitionSpec as P

MESH = pl.DeviceIdType.MESH
HEAD = 128
QPK = 4
ROWS = 256
PAGE = 16
COLS = 1024
SLOTS = 64
NPAGES = 512
NEG = -1e30
SCALE2 = 128.0 ** -0.5 * 1.4426950408889634

Z_SET = (1, 3, 4, 5, 7, 8, 9, 10, 12, 13, 15)
X_SET = (2, 6, 11, 14)
N_SET = 16

Y_ROWS = (64, 64, 32)
X_ROWS = (48, 48)
Y_FIRST, X_FIRST = len(Y_ROWS), len(X_ROWS)
NEAR = sum(Y_ROWS)
ORDER = (
    ("p", 2, 1), ("sn", 0, 0, 0), ("sn", 0, 1, 0), ("sx", 0, 2), ("p", 1, 1), ("sn", 0, 0, 1),
    ("sa", 0), ("sn", 1, 0, 0), ("sn", 1, 0, 1), ("sn", 2, 0, 0), ("sn", 2, 0, 1), ("sx", 0, 1), ("p", 3, 1),
    ("sn", 0, 1, 1), ("sa", 1), ("sn", 1, 1, 0), ("sn", 1, 1, 1), ("sn", 2, 1, 0), ("sn", 2, 1, 1),
    ("sx", 0, 3), ("p", 0, 1), ("sx", 0, 0), ("sx", 1, 2), ("sx", 1, 1), ("sx", 1, 3), ("sx", 1, 0),
    ("p", 2, 0), ("p", 1, 0), ("p", 3, 0), ("p", 0, 0), ("forward",), ("pages", 0), ("pages", 1), ("wm", 0, 2),
    ("na", 0, 0), ("na", 0, 1), ("pages", 2), ("pages", 3), ("wm", 0, 1), ("sum", 0), ("wm", 0, 3),
    ("relay", 0), ("relay", 1), ("na", 1, 0), ("na", 1, 1), ("sum", 1), ("sum", 2), ("wm", 1, 2), ("na", 2, 0), ("na", 2, 1),
    ("wa", 0, 0), ("wa", 0, 1), ("wm", 1, 1), ("nc", 0), ("sum", 3), ("wm", 1, 3), ("nc", 1), ("wa", 1, 0), ("wa", 1, 1),
    ("nc", 2), ("wo", 0), ("no", 0), ("wo", 1), ("no", 1), ("no", 2),
)


def plus_slot(r):
    return 4 * Z_SET[r]


def minus_slot(r):
    return 4 * Z_SET[r] + 1


def x_slot(i):
    return 4 * X_SET[i // 2] + i % 2


def half_blocks(z, xl, c):
    def index(dz, other, flip):
        return lax.rem(z + dz + 8, 8) * 4 + (1 - xl if other else xl) * 2 + (1 - c if flip else c)

    found = []
    for flip in (0, 1):
        at = 2 * flip
        found += [(at, index(0, 0, flip), 0), (at + 1, index(0, 0, flip), 1)]
        for r in range(11):
            d = r // 3 + 1
            if r < 9:
                half, other = ((0, 0), (1, 0), (0, 1))[r % 3]
            else:
                half, other = (0, r - 9)
            found.append((plus_slot(r) + at, index(-d, other, flip), half))
            if r < 9:
                half, other = ((1, 0), (0, 0), (0, 1))[r % 3]
            else:
                half, other = (1, r - 9)
            found.append((minus_slot(r) + at, index(d, other, flip), half))
        for i, (dz, half) in enumerate(((0, 0), (0, 1), (1, 1), (-1, 1), (2, 1), (-2, 1), (3, 1), (-3, 1))):
            found.append((x_slot(i) + at, index(dz, 1, flip), half))
    return found


def kernel(order_hbm, owner_hbm, q_hbm, k_hbm, v_hbm, w_hbm, out_ref, pages_ref,
           slices, gathered, own, order_ref, owner_ref, kv, q_raw, qx, top, acc, att, w, part, uy, ux, wx, wy, table_v, table_s, place, holder,
           load_sem, w_sem, z_ssem, z_rsem, x_ssem, x_rsem, d_ssem, d_rsem,
           slice_ssem, slice_rsem, half_ssem, half_rsem, att_ssem, att_rsem,
           uy_ssem, uy_rsem, ux_ssem, ux_rsem, wx_ssem, wx_rsem, wy_ssem, wy_rsem):
    grp, tp = lax.axis_index("grp"), lax.axis_index("tp")
    z, xl, c = grp // 4, lax.rem(grp // 2, 2), lax.rem(grp, 2)
    y, xh = tp // 2, lax.rem(tp, 2)

    def at_grp(z_to, xl_to, c_to):
        return (z_to * 4 + xl_to * 2 + c_to, tp)

    z_up = at_grp(lax.rem(z + 1, 8), xl, c)
    z_down = at_grp(lax.rem(z + 7, 8), xl, c)
    x_near = at_grp(z, 1 - xl, c)
    core = at_grp(z, xl, 1 - c)
    y_up = (grp, lax.rem(y + 1, 4) * 2 + xh)
    y_down = (grp, lax.rem(y + 3, 4) * 2 + xh)
    y_far = (grp, lax.rem(y + 2, 4) * 2 + xh)
    x_far = (grp, y * 2 + 1 - xh)

    barrier = pltpu.get_barrier_semaphore()
    for near in (z_up, z_down, x_near, core, y_up, y_down, y_far, x_far):
        pl.semaphore_signal(barrier, inc=1, device_id=near, device_id_type=MESH)

    loads = []
    for half in range(2):
        for ref, lane in ((k_hbm, 0), (v_hbm, HEAD)):
            loads.append(pltpu.make_async_copy(
                ref.at[pl.ds(8 * half, 8)], kv.at[pl.ds(8 * half, 8), :, pl.ds(lane, HEAD)],
                load_sem.at[len(loads)]))
    load_q = pltpu.make_async_copy(q_hbm, q_raw, load_sem.at[4])
    load_w = pltpu.make_async_copy(w_hbm, w, w_sem)
    for load in loads:
        load.start()
    load_order = pltpu.make_async_copy(order_hbm, order_ref, load_sem.at[6])
    load_owner = pltpu.make_async_copy(owner_hbm, owner_ref, load_sem.at[7])
    load_order.start()
    load_owner.start()
    load_q.start()
    load_w.start()

    for slot, block, half in half_blocks(z, xl, c):
        place[2 * block + half] = slot + 0 * grp
        holder[slot] = block

    for load in loads:
        load.wait()
    pl.semaphore_wait(barrier, 8)

    sent = []

    def remote(src, dst, ssem, rsem, to):
        return pltpu.make_async_remote_copy(src_ref=src, dst_ref=dst, send_sem=ssem, recv_sem=rsem,
                                            device_id=to, device_id_type=MESH)

    def slots(first, count=1):
        return kv.at[pl.ds(8 * first, 8 * count)]

    def plus(r, src):
        return remote(slots(src), slots(plus_slot(r)), z_ssem.at[0, r], z_rsem.at[0, r], z_up)

    def minus(r, src):
        return remote(slots(src), slots(minus_slot(r)), z_ssem.at[1, r], z_rsem.at[1, r], z_down)

    def cross(i, src):
        return remote(slots(src), slots(x_slot(i)), x_ssem.at[i], x_rsem.at[i], x_near)

    def twin(k):
        return remote(slots(4 * k, 2), slots(4 * k + 2, 2), d_ssem.at[k], d_rsem.at[k], core)

    def begin(make, *which):
        make(*which).start()
        sent.append((make, which))

    begin(cross, 0, 0)
    begin(plus, 0, 0)
    begin(minus, 0, 1)
    begin(twin, 0)
    begin(cross, 1, 1)
    begin(plus, 1, 1)
    begin(minus, 1, 0)

    ahead = (y_up, y_down, y_far)
    steps = (1, 3, 2)

    def weight_slice(n):
        first = (lax.rem(y + steps[n], 4) * 2 + xh) * COLS
        src = w_hbm.at[pl.ds(pl.multiple_of(256 * c, 256), 256), pl.ds(pl.multiple_of(first, COLS), COLS)]
        return remote(src, slices.at[n, pl.ds(pl.multiple_of(256 * c, 256), 256)],
                      slice_ssem.at[n], slice_rsem.at[n], ahead[n])

    def weight_half(n):
        half = slices.at[n, pl.ds(pl.multiple_of(256 * c, 256), 256)]
        return remote(half, half, half_ssem.at[n], half_rsem.at[n], core)

    for n in range(3):
        begin(weight_slice, n)

    def z_step(r):
        plus(r, 0).wait_recv()
        minus(r, 0).wait_recv()
        if r <= 6:
            begin(plus, r + 3, plus_slot(r))
            begin(minus, r + 3, minus_slot(r))
        if r == 8:
            begin(plus, 10, plus_slot(8))
        if r % 3 == 0 and r <= 6:
            begin(cross, 2 + 2 * (r // 3), minus_slot(r))
        if r % 3 == 1 and r <= 7:
            begin(cross, 3 + 2 * (r // 3), plus_slot(r))
        begin(twin, Z_SET[r])

    def x_step(i):
        cross(i, 0).wait_recv()
        if i == 0:
            begin(plus, 2, x_slot(0))
            begin(minus, 2, x_slot(0))
        if i == 6:
            begin(minus, 10, x_slot(6))
        if i % 2 == 1:
            begin(twin, X_SET[i // 2])

    before = {
        1: (("x", 0), ("z", 0), ("x", 1), ("z", 1)),
        3: (("z", 2), ("x", 2)),
        4: (("z", 3), ("x", 3)),
        5: (("z", 4),),
        6: (("z", 5),),
        7: (("z", 6), ("x", 4)),
        8: (("x", 5), ("z", 7)),
        10: (("z", 8), ("x", 6)),
        11: (("z", 9),),
        12: (("x", 7),),
        13: (("z", 10),),
    }

    def softmax_step(k, first):
        block = kv[pl.ds(32 * k, 32)].reshape(512, 2 * HEAD)
        rows = []
        for j in range(4):
            seen = order_ref[holder[4 * k + j]] < here
            if first and j < 2:
                seen = True
            rows.append(jnp.full((HEAD, HEAD), jnp.where(seen, 0.0, NEG), jnp.float32).astype(jnp.bfloat16))
        keys = jnp.concatenate([block[:, :HEAD], jnp.concatenate(rows, axis=0)], axis=1)
        values = jnp.concatenate([block[:, HEAD:], jnp.ones((512, HEAD), jnp.bfloat16)], axis=1)
        scores = [lax.dot_general(qx[h], keys, (((1,), (1,)), ((), ())), preferred_element_type=jnp.float32)
                  for h in range(QPK)]
        for h in range(QPK):
            tiles = [scores[h][:, HEAD * j:HEAD * (j + 1)] for j in range(4)]
            if first:
                row = lax.broadcasted_iota(jnp.int32, (ROWS, HEAD), 0)
                lane = lax.broadcasted_iota(jnp.int32, (ROWS, HEAD), 1)
                for j in range(2):
                    tiles[j] = jnp.where(lane + HEAD * j <= row, tiles[j], NEG)
            peak = jnp.max(jnp.maximum(jnp.maximum(tiles[0], tiles[1]), jnp.maximum(tiles[2], tiles[3])),
                           axis=1, keepdims=True)
            if first:
                new = jnp.broadcast_to(peak, (ROWS, HEAD))
            else:
                old = top[h]
                new = jnp.maximum(old, peak)
            expo = [jnp.exp2((tile - new) * SCALE2).astype(jnp.bfloat16) for tile in tiles]
            gained = jnp.dot(jnp.concatenate(expo, axis=1), values, preferred_element_type=jnp.float32)
            top[h] = new
            if first:
                acc[h] = gained
            else:
                factor = jnp.exp2((old - new) * SCALE2)
                acc[h] = acc[h] * jnp.concatenate([factor, factor], axis=1) + gained

    load_order.wait()
    load_owner.wait()
    here = order_ref[grp]
    load_q.wait()
    lane = lax.broadcasted_iota(jnp.int32, (ROWS, HEAD), 1)
    unit = jnp.where(lane == 0, 1.0, 0.0).astype(jnp.bfloat16)
    for h in range(QPK):
        qx[h] = jnp.concatenate([q_raw[:, HEAD * h:HEAD * (h + 1)], unit], axis=1)
    twin(0).wait_recv()
    softmax_step(0, True)

    @pl.loop(1, N_SET)
    def _(k):
        for at, events in before.items():
            @pl.when(k == at)
            def _():
                for kind, r in events:
                    (z_step if kind == "z" else x_step)(r)
        twin(k).wait_recv()
        softmax_step(k, False)

    for h in range(QPK):
        att[:, HEAD * h:HEAD * (h + 1)] = (acc[h, :, :HEAD] / acc[h, :, HEAD:]).astype(jnp.bfloat16)
    load_w.wait()

    def cols_of(i, j):
        return (lax.rem(y + i, 4) * 2 + (1 - xh if j else xh)) * COLS

    def project(i, j):
        rows = pl.ds(0, ROWS) if j else pl.ds(NEAR, ROWS - NEAR)
        for n in range(2):
            at = pl.multiple_of(cols_of(i, j) + n * 512, 512)
            part[i, j, rows, pl.ds(n * 512, 512)] = jnp.dot(
                att[rows], w[:, pl.ds(at, 512)], preferred_element_type=jnp.float32).astype(jnp.bfloat16)

    def u_rows(g):
        return pl.ds(sum(Y_ROWS[:g]), Y_ROWS[g])

    def w_rows(g):
        return pl.ds(NEAR + sum(X_ROWS[:g]), X_ROWS[g])

    def att_rows(n):
        return remote(att.at[pl.ds(0, NEAR)], gathered.at[n], att_ssem.at[n], att_rsem.at[n], ahead[n])

    def att_relay(way):
        half = pl.ds(NEAR // 2 * way, NEAR // 2)
        return remote(gathered.at[way, half], gathered.at[2, half], att_ssem.at[2 + way], att_rsem.at[2 + way],
                      ahead[way])

    def relay(way):
        att_rows(way).wait_recv()
        begin(att_relay, way)

    def along_y(way, n, j, rows, to, ssem, rsem):
        i = (2, 1, 1)[n] if way == 0 else (2, 3, 3)[n]
        left = (0, 1, 0)[n] if way == 0 else (1, 0, 1)[n]
        return remote(part.at[i, j, rows, pl.ds(512 * left, 512)], to, ssem, rsem, (y_up, y_down)[way])

    def u_near(g, way, n):
        return along_y(way, n, 1, u_rows(g), uy.at[g, way, n, pl.ds(0, Y_ROWS[g])],
                       uy_ssem.at[g, way, n], uy_rsem.at[g, way, n])

    def w_near(g, way, n):
        return along_y(way, n, 0, w_rows(g), wy.at[g, way, n, pl.ds(0, X_ROWS[g])],
                       wy_ssem.at[g, way, n], wy_rsem.at[g, way, n])

    def u_far(g):
        return remote(part.at[0, 1, u_rows(g)], ux.at[g, pl.ds(0, Y_ROWS[g])], ux_ssem.at[g], ux_rsem.at[g], x_far)

    def w_far(g, i):
        return remote(part.at[i, 1, w_rows(g)], wx.at[g, i, pl.ds(0, X_ROWS[g])],
                      wx_ssem.at[g, i], wx_rsem.at[g, i], x_far)

    def wide(a):
        return a.astype(jnp.float32)

    def add_half(near, j, rows, came, g, way):
        i, cols = (1, 3)[way], pl.ds(512 * way, 512)
        near(g, way, 0).wait_recv()
        part[i, j, rows, cols] = (wide(part[i, j, rows, cols]) + wide(came())).astype(jnp.bfloat16)
        begin(near, g, way, 2)

    def both_ways(near, g):
        for way in (0, 1):
            for n in (1, 2):
                near(g, way, n).wait_recv()

    def came_along_y(buf, g, size):
        return jnp.concatenate([wide(buf[g, 0, 2 - left, :size]) + wide(buf[g, 1, 1 + left, :size])
                                for left in (0, 1)], axis=1)

    def u_add(g, way):
        add_half(u_near, 1, u_rows(g), lambda: uy[g, way, 0, :Y_ROWS[g]], g, way)

    def u_cross(g):
        both_ways(u_near, g)
        part[0, 1, u_rows(g)] = (wide(part[0, 1, u_rows(g)]) + came_along_y(uy, g, Y_ROWS[g])).astype(jnp.bfloat16)
        begin(u_far, g)

    def u_out(g):
        u_far(g).wait_recv()
        out_ref[u_rows(g)] = (own[u_rows(g)] + wide(ux[g, :Y_ROWS[g]])).astype(jnp.bfloat16)

    def forward():
        for n in range(3):
            weight_slice(n).wait_recv()
            begin(weight_half, n)

    def own_sum(n):
        if n == 0:
            at = pl.multiple_of(cols_of(0, 0), COLS)
            own[...] = jnp.dot(att[pl.ds(0, NEAR)], w[:, pl.ds(at, COLS)], preferred_element_type=jnp.float32)
        else:
            if n == 3:
                att_relay(0).wait_recv()
                att_relay(1).wait_recv()
            weight_half(n - 1).wait_recv()
            own[...] += jnp.dot(gathered[n - 1], slices[n - 1], preferred_element_type=jnp.float32)

    def w_mid(g, i):
        at = w_rows(g)
        w_far(g, i).wait_recv()
        part[i, 0, at] = (wide(part[i, 0, at]) + wide(wx[g, i, :X_ROWS[g]])).astype(jnp.bfloat16)
        if i == 2:
            begin(w_near, g, 0, 0)
            begin(w_near, g, 1, 0)
        else:
            begin(w_near, g, (1 if i == 3 else 0), 1)

    def w_add(g, way):
        add_half(w_near, 0, w_rows(g), lambda: wy[g, way, 0, :X_ROWS[g]], g, way)

    def w_out(g):
        at, size = w_rows(g), X_ROWS[g]
        w_far(g, 0).wait_recv()
        both_ways(w_near, g)
        total = wide(part[0, 0, at]) + wide(wx[g, 0, :size]) + came_along_y(wy, g, size)
        out_ref[at] = total.astype(jnp.bfloat16)

    def find_pages():
        lanes = lax.broadcasted_iota(jnp.int32, (8, 128), 1)

        def look(i, carry):
            found, count = carry
            mine = owner_ref[i] == grp
            found = jnp.where((lanes == count) & mine, i, found)
            return found, count + jnp.where(mine, 1, 0)

        found, count = lax.fori_loop(0, NPAGES, look, (jnp.zeros((8, 128), jnp.int32), 0 * grp), unroll=8)
        table_v[...] = found
        fetch = pltpu.make_async_copy(table_v, table_s, load_sem.at[5])
        fetch.start()
        fetch.wait()
        return count

    def hand_pages(first, count):
        @pl.loop(first, first + SLOTS // 4)
        def _(s):
            page = table_s[0, s]
            slot = place[page // 8]
            rows = kv[slot * 8 + lax.rem(page, 8)]
            pages_ref[s] = jnp.where(s < count, rows, jnp.zeros_like(rows))

    owned = 0
    for step, *which in ORDER:
        if step == "p":
            project(*which)
        elif step in ("sa", "sn", "sx"):
            begin({"sa": att_rows, "sn": u_near, "sx": w_far}[step], *which)
        elif step == "pages":
            if which[0] == 0:
                owned = find_pages()
            hand_pages(which[0] * (SLOTS // 4), owned)
        else:
            {"na": u_add, "nc": u_cross, "no": u_out, "wm": w_mid, "wa": w_add, "wo": w_out,
             "forward": forward, "relay": relay, "sum": own_sum}[step](*which)

    for make, which in sent:
        make(*which).wait_send()


def on_device(queries, key_rows, value_rows, out_weight, block_order, page_owner):
    dma = pltpu.SemaphoreType.DMA
    vmem = pltpu.VMEM
    bf16, f32, i32 = jnp.bfloat16, jnp.float32, jnp.int32
    hbm = pl.BlockSpec(memory_space=pltpu.HBM)
    vmem_out = pl.BlockSpec(memory_space=pltpu.VMEM)
    made = pl.pallas_call(
        kernel,
        name="attend",
        out_shape=(vmem((ROWS, COLS), bf16), vmem((SLOTS, PAGE, 2 * HEAD), bf16)),
        in_specs=[hbm] * 6,
        out_specs=(vmem_out, vmem_out),
        scratch_shapes=[
            vmem((3, QPK * HEAD, COLS), bf16),
            vmem((3, NEAR, QPK * HEAD), bf16),
            vmem((NEAR, COLS), f32),
            pltpu.SMEM((32,), i32),
            pltpu.SMEM((NPAGES,), i32),
            vmem((NPAGES, PAGE, 2 * HEAD), bf16),
            vmem((ROWS, QPK * HEAD), bf16),
            vmem((QPK, ROWS, 2 * HEAD), bf16),
            vmem((QPK, ROWS, HEAD), f32),
            vmem((QPK, ROWS, 2 * HEAD), f32),
            vmem((ROWS, QPK * HEAD), bf16),
            vmem((QPK * HEAD, 8 * COLS), bf16),
            vmem((4, 2, ROWS, COLS), bf16),
            vmem((Y_FIRST, 2, 3, max(Y_ROWS), COLS // 2), bf16),
            vmem((Y_FIRST, max(Y_ROWS), COLS), bf16),
            vmem((X_FIRST, 4, max(X_ROWS), COLS), bf16),
            vmem((X_FIRST, 2, 3, max(X_ROWS), COLS // 2), bf16),
            vmem((8, 128), i32),
            pltpu.SMEM((8, 128), i32),
            pltpu.SMEM((64,), i32),
            pltpu.SMEM((64,), i32),
            dma((8,)), dma,
            dma((2, 11)), dma((2, 11)), dma((8,)), dma((8,)), dma((N_SET,)), dma((N_SET,)),
            dma((3,)), dma((3,)), dma((3,)), dma((3,)), dma((4,)), dma((4,)),
            dma((Y_FIRST, 2, 3)), dma((Y_FIRST, 2, 3)), dma((Y_FIRST,)), dma((Y_FIRST,)),
            dma((X_FIRST, 4)), dma((X_FIRST, 4)), dma((X_FIRST, 2, 3)), dma((X_FIRST, 2, 3)),
        ],
        compiler_params=pltpu.CompilerParams(
            collective_id=0, has_side_effects=True, vmem_limit_bytes=56 * 2**20),
    )(block_order, page_owner.reshape(NPAGES), queries,
      key_rows.reshape(PAGE, PAGE, HEAD), value_rows.reshape(PAGE, PAGE, HEAD), out_weight)
    return made


def solution(mesh):
    placed = (P("grp", "tp"), P("grp", "tp"), P("grp", "tp"), P("tp", None), P(), P())
    return jax.shard_map(
        on_device,
        mesh=mesh,
        in_specs=placed,
        out_specs=(P("grp", "tp"), P("grp", None, "tp")),
        check_vma=False,
    )
```

```python
import functools

import jax
import jax.numpy as jnp
from jax import lax
from jax.experimental import pallas as pl
from jax.experimental.pallas import tpu as pltpu
from jax.sharding import PartitionSpec as P

MESH = pl.DeviceIdType.MESH
HEAD = 128
QPK = 4
ROWS = 256
PAGE = 16
COLS = 1024
SLOTS = 64
NPAGES = 512
NEG = -1e30
SCALE2 = 128.0 ** -0.5 * 1.4426950408889634

Z_SET = (1, 3, 4, 5, 7, 8, 9, 10, 12, 13, 15)
X_SET = (2, 6, 11, 14)
N_SET = 16

Y_ROWS = (64, 64, 32)
X_ROWS = (48, 48)
Y_FIRST, X_FIRST = len(Y_ROWS), len(X_ROWS)
NEAR = sum(Y_ROWS)
ORDER = (
    ("sa", 0), ("sa", 1),
    ("p", 2, 1), ("sn", 0, 0, 0), ("sn", 0, 1, 0), ("sx", 0, 2), ("p", 1, 1), ("sn", 0, 0, 1),
    ("sn", 1, 0, 0), ("sn", 1, 0, 1), ("sn", 2, 0, 0), ("sn", 2, 0, 1), ("sx", 0, 1), ("p", 3, 1),
    ("sn", 0, 1, 1), ("sn", 1, 1, 0), ("sn", 1, 1, 1), ("sn", 2, 1, 0), ("sn", 2, 1, 1),
    ("sx", 0, 3), ("p", 0, 1), ("sx", 0, 0), ("sx", 1, 2), ("sx", 1, 1), ("sx", 1, 3), ("sx", 1, 0),
    ("p", 2, 0), ("p", 1, 0), ("p", 3, 0), ("p", 0, 0), ("forward",), ("pages", 0), ("pages", 1), ("wm", 0, 2),
    ("na", 0, 0), ("na", 0, 1), ("pages", 2), ("pages", 3), ("wm", 0, 1), ("sum", 0), ("wm", 0, 3),
    ("relay", 0), ("relay", 1), ("na", 1, 0), ("na", 1, 1), ("sum", 1), ("sum", 2), ("wm", 1, 2), ("na", 2, 0), ("na", 2, 1),
    ("wa", 0, 0), ("wa", 0, 1), ("wm", 1, 1), ("nc", 0), ("sum", 3), ("wm", 1, 3), ("nc", 1), ("wa", 1, 0), ("wa", 1, 1),
    ("nc", 2), ("wo", 0), ("no", 0), ("wo", 1), ("no", 1), ("no", 2),
)


def plus_slot(r):
    return 4 * Z_SET[r]


def minus_slot(r):
    return 4 * Z_SET[r] + 1


def x_slot(i):
    return 4 * X_SET[i // 2] + i % 2


def half_blocks(z, xl, c):
    def index(dz, other, flip):
        return lax.rem(z + dz + 8, 8) * 4 + (1 - xl if other else xl) * 2 + (1 - c if flip else c)

    found = []
    for flip in (0, 1):
        at = 2 * flip
        found += [(at, index(0, 0, flip), 0), (at + 1, index(0, 0, flip), 1)]
        for r in range(11):
            d = r // 3 + 1
            if r < 9:
                half, other = ((0, 0), (1, 0), (0, 1))[r % 3]
            else:
                half, other = (0, r - 9)
            found.append((plus_slot(r) + at, index(-d, other, flip), half))
            if r < 9:
                half, other = ((1, 0), (0, 0), (0, 1))[r % 3]
            else:
                half, other = (1, r - 9)
            found.append((minus_slot(r) + at, index(d, other, flip), half))
        for i, (dz, half) in enumerate(((0, 0), (0, 1), (1, 1), (-1, 1), (2, 1), (-2, 1), (3, 1), (-3, 1))):
            found.append((x_slot(i) + at, index(dz, 1, flip), half))
    return found


def kernel(order_hbm, owner_hbm, q_hbm, k_hbm, v_hbm, w_hbm, out_ref, pages_ref,
           slices, gathered, own, order_ref, owner_ref, kv, q_raw, qx, top, acc, att, w, part, uy, ux, wx, wy, table_v, table_s, place, holder,
           load_sem, w_sem, z_ssem, z_rsem, x_ssem, x_rsem, d_ssem, d_rsem,
           slice_ssem, slice_rsem, half_ssem, half_rsem, att_ssem, att_rsem,
           uy_ssem, uy_rsem, ux_ssem, ux_rsem, wx_ssem, wx_rsem, wy_ssem, wy_rsem):
    grp, tp = lax.axis_index("grp"), lax.axis_index("tp")
    z, xl, c = grp // 4, lax.rem(grp // 2, 2), lax.rem(grp, 2)
    y, xh = tp // 2, lax.rem(tp, 2)

    def at_grp(z_to, xl_to, c_to):
        return (z_to * 4 + xl_to * 2 + c_to, tp)

    z_up = at_grp(lax.rem(z + 1, 8), xl, c)
    z_down = at_grp(lax.rem(z + 7, 8), xl, c)
    x_near = at_grp(z, 1 - xl, c)
    core = at_grp(z, xl, 1 - c)
    y_up = (grp, lax.rem(y + 1, 4) * 2 + xh)
    y_down = (grp, lax.rem(y + 3, 4) * 2 + xh)
    y_far = (grp, lax.rem(y + 2, 4) * 2 + xh)
    x_far = (grp, y * 2 + 1 - xh)

    barrier = pltpu.get_barrier_semaphore()
    for near in (z_up, z_down, x_near, core, y_up, y_down, y_far, x_far):
        pl.semaphore_signal(barrier, inc=1, device_id=near, device_id_type=MESH)

    loads = []
    for half in range(2):
        for ref, lane in ((k_hbm, 0), (v_hbm, HEAD)):
            loads.append(pltpu.make_async_copy(
                ref.at[pl.ds(8 * half, 8)], kv.at[pl.ds(8 * half, 8), :, pl.ds(lane, HEAD)],
                load_sem.at[len(loads)]))
    load_q = pltpu.make_async_copy(q_hbm, q_raw, load_sem.at[4])
    load_w = pltpu.make_async_copy(w_hbm, w, w_sem)
    for load in loads:
        load.start()
    load_order = pltpu.make_async_copy(order_hbm, order_ref, load_sem.at[6])
    load_owner = pltpu.make_async_copy(owner_hbm, owner_ref, load_sem.at[7])
    load_order.start()
    load_owner.start()
    load_q.start()
    load_w.start()

    for slot, block, half in half_blocks(z, xl, c):
        place[2 * block + half] = slot + 0 * grp
        holder[slot] = block

    for load in loads:
        load.wait()
    pl.semaphore_wait(barrier, 8)

    sent = []

    def remote(src, dst, ssem, rsem, to):
        return pltpu.make_async_remote_copy(src_ref=src, dst_ref=dst, send_sem=ssem, recv_sem=rsem,
                                            device_id=to, device_id_type=MESH)

    def slots(first, count=1):
        return kv.at[pl.ds(8 * first, 8 * count)]

    def plus(r, src):
        return remote(slots(src), slots(plus_slot(r)), z_ssem.at[0, r], z_rsem.at[0, r], z_up)

    def minus(r, src):
        return remote(slots(src), slots(minus_slot(r)), z_ssem.at[1, r], z_rsem.at[1, r], z_down)

    def cross(i, src):
        return remote(slots(src), slots(x_slot(i)), x_ssem.at[i], x_rsem.at[i], x_near)

    def twin(k):
        return remote(slots(4 * k, 2), slots(4 * k + 2, 2), d_ssem.at[k], d_rsem.at[k], core)

    def begin(make, *which):
        make(*which).start()
        sent.append((make, which))

    begin(cross, 0, 0)
    begin(plus, 0, 0)
    begin(minus, 0, 1)
    begin(twin, 0)
    begin(cross, 1, 1)
    begin(plus, 1, 1)
    begin(minus, 1, 0)

    ahead = (y_up, y_down, y_far)
    steps = (1, 3, 2)

    def weight_slice(n):
        first = (lax.rem(y + steps[n], 4) * 2 + xh) * COLS
        src = w_hbm.at[pl.ds(pl.multiple_of(256 * c, 256), 256), pl.ds(pl.multiple_of(first, COLS), COLS)]
        return remote(src, slices.at[n, pl.ds(pl.multiple_of(256 * c, 256), 256)],
                      slice_ssem.at[n], slice_rsem.at[n], ahead[n])

    def weight_half(n):
        half = slices.at[n, pl.ds(pl.multiple_of(256 * c, 256), 256)]
        return remote(half, half, half_ssem.at[n], half_rsem.at[n], core)

    for n in range(3):
        begin(weight_slice, n)

    def z_step(r):
        plus(r, 0).wait_recv()
        minus(r, 0).wait_recv()
        if r <= 6:
            begin(plus, r + 3, plus_slot(r))
            begin(minus, r + 3, minus_slot(r))
        if r == 8:
            begin(plus, 10, plus_slot(8))
        if r % 3 == 0 and r <= 6:
            begin(cross, 2 + 2 * (r // 3), minus_slot(r))
        if r % 3 == 1 and r <= 7:
            begin(cross, 3 + 2 * (r // 3), plus_slot(r))
        begin(twin, Z_SET[r])

    def x_step(i):
        cross(i, 0).wait_recv()
        if i == 0:
            begin(plus, 2, x_slot(0))
            begin(minus, 2, x_slot(0))
        if i == 6:
            begin(minus, 10, x_slot(6))
        if i % 2 == 1:
            begin(twin, X_SET[i // 2])

    before = {
        1: (("x", 0), ("z", 0), ("x", 1), ("z", 1)),
        3: (("z", 2), ("x", 2)),
        4: (("z", 3), ("x", 3)),
        5: (("z", 4),),
        6: (("z", 5),),
        7: (("z", 6), ("x", 4)),
        8: (("x", 5), ("z", 7)),
        10: (("z", 8), ("x", 6)),
        11: (("z", 9),),
        12: (("x", 7),),
        13: (("z", 10),),
    }

    def softmax_step(k, first):
        block = kv[pl.ds(32 * k, 32)].reshape(512, 2 * HEAD)
        rows = []
        for j in range(4):
            seen = order_ref[holder[4 * k + j]] < here
            if first and j < 2:
                seen = True
            rows.append(jnp.full((HEAD, HEAD), jnp.where(seen, 0.0, NEG), jnp.float32).astype(jnp.bfloat16))
        keys = jnp.concatenate([block[:, :HEAD], jnp.concatenate(rows, axis=0)], axis=1)
        values = jnp.concatenate([block[:, HEAD:], jnp.ones((512, HEAD), jnp.bfloat16)], axis=1)
        scores = [lax.dot_general(qx[h], keys, (((1,), (1,)), ((), ())), preferred_element_type=jnp.float32)
                  for h in range(QPK)]
        for h in range(QPK):
            tiles = [scores[h][:, HEAD * j:HEAD * (j + 1)] for j in range(4)]
            if first:
                row = lax.broadcasted_iota(jnp.int32, (ROWS, HEAD), 0)
                lane = lax.broadcasted_iota(jnp.int32, (ROWS, HEAD), 1)
                for j in range(2):
                    tiles[j] = jnp.where(lane + HEAD * j <= row, tiles[j], NEG)
            peak = jnp.max(jnp.maximum(jnp.maximum(tiles[0], tiles[1]), jnp.maximum(tiles[2], tiles[3])),
                           axis=1, keepdims=True)
            if first:
                new = jnp.broadcast_to(peak, (ROWS, HEAD))
            else:
                old = top[h]
                new = jnp.maximum(old, peak)
            expo = [jnp.exp2((tile - new) * SCALE2).astype(jnp.bfloat16) for tile in tiles]
            gained = jnp.dot(jnp.concatenate(expo, axis=1), values, preferred_element_type=jnp.float32)
            top[h] = new
            if first:
                acc[h] = gained
            else:
                factor = jnp.exp2((old - new) * SCALE2)
                acc[h] = acc[h] * jnp.concatenate([factor, factor], axis=1) + gained

    load_order.wait()
    load_owner.wait()
    here = order_ref[grp]
    load_q.wait()
    lane = lax.broadcasted_iota(jnp.int32, (ROWS, HEAD), 1)
    unit = jnp.where(lane == 0, 1.0, 0.0).astype(jnp.bfloat16)
    for h in range(QPK):
        qx[h] = jnp.concatenate([q_raw[:, HEAD * h:HEAD * (h + 1)], unit], axis=1)
    twin(0).wait_recv()
    softmax_step(0, True)

    @pl.loop(1, N_SET)
    def _(k):
        for at, events in before.items():
            @pl.when(k == at)
            def _():
                for kind, r in events:
                    (z_step if kind == "z" else x_step)(r)
        twin(k).wait_recv()
        softmax_step(k, False)

    for h in range(QPK):
        att[:, HEAD * h:HEAD * (h + 1)] = (acc[h, :, :HEAD] / acc[h, :, HEAD:]).astype(jnp.bfloat16)
    load_w.wait()

    def cols_of(i, j):
        return (lax.rem(y + i, 4) * 2 + (1 - xh if j else xh)) * COLS

    def project(i, j):
        rows = pl.ds(0, ROWS) if j else pl.ds(NEAR, ROWS - NEAR)
        for n in range(2):
            at = pl.multiple_of(cols_of(i, j) + n * 512, 512)
            part[i, j, rows, pl.ds(n * 512, 512)] = jnp.dot(
                att[rows], w[:, pl.ds(at, 512)], preferred_element_type=jnp.float32).astype(jnp.bfloat16)

    def u_rows(g):
        return pl.ds(sum(Y_ROWS[:g]), Y_ROWS[g])

    def w_rows(g):
        return pl.ds(NEAR + sum(X_ROWS[:g]), X_ROWS[g])

    def att_rows(n):
        return remote(att.at[pl.ds(0, NEAR)], gathered.at[n], att_ssem.at[n], att_rsem.at[n], ahead[n])

    def att_relay(way):
        half = pl.ds(NEAR // 2 * way, NEAR // 2)
        return remote(gathered.at[way, half], gathered.at[2, half], att_ssem.at[2 + way], att_rsem.at[2 + way],
                      ahead[way])

    def relay(way):
        att_rows(way).wait_recv()
        begin(att_relay, way)

    def along_y(way, n, j, rows, to, ssem, rsem):
        i = (2, 1, 1)[n] if way == 0 else (2, 3, 3)[n]
        left = (0, 1, 0)[n] if way == 0 else (1, 0, 1)[n]
        return remote(part.at[i, j, rows, pl.ds(512 * left, 512)], to, ssem, rsem, (y_up, y_down)[way])

    def u_near(g, way, n):
        return along_y(way, n, 1, u_rows(g), uy.at[g, way, n, pl.ds(0, Y_ROWS[g])],
                       uy_ssem.at[g, way, n], uy_rsem.at[g, way, n])

    def w_near(g, way, n):
        return along_y(way, n, 0, w_rows(g), wy.at[g, way, n, pl.ds(0, X_ROWS[g])],
                       wy_ssem.at[g, way, n], wy_rsem.at[g, way, n])

    def u_far(g):
        return remote(part.at[0, 1, u_rows(g)], ux.at[g, pl.ds(0, Y_ROWS[g])], ux_ssem.at[g], ux_rsem.at[g], x_far)

    def w_far(g, i):
        return remote(part.at[i, 1, w_rows(g)], wx.at[g, i, pl.ds(0, X_ROWS[g])],
                      wx_ssem.at[g, i], wx_rsem.at[g, i], x_far)

    def wide(a):
        return a.astype(jnp.float32)

    def add_half(near, j, rows, came, g, way):
        i, cols = (1, 3)[way], pl.ds(512 * way, 512)
        near(g, way, 0).wait_recv()
        part[i, j, rows, cols] = (wide(part[i, j, rows, cols]) + wide(came())).astype(jnp.bfloat16)
        begin(near, g, way, 2)

    def both_ways(near, g):
        for way in (0, 1):
            for n in (1, 2):
                near(g, way, n).wait_recv()

    def came_along_y(buf, g, size):
        return jnp.concatenate([wide(buf[g, 0, 2 - left, :size]) + wide(buf[g, 1, 1 + left, :size])
                                for left in (0, 1)], axis=1)

    def u_add(g, way):
        add_half(u_near, 1, u_rows(g), lambda: uy[g, way, 0, :Y_ROWS[g]], g, way)

    def u_cross(g):
        both_ways(u_near, g)
        part[0, 1, u_rows(g)] = (wide(part[0, 1, u_rows(g)]) + came_along_y(uy, g, Y_ROWS[g])).astype(jnp.bfloat16)
        begin(u_far, g)

    def u_out(g):
        u_far(g).wait_recv()
        out_ref[u_rows(g)] = (own[u_rows(g)] + wide(ux[g, :Y_ROWS[g]])).astype(jnp.bfloat16)

    def forward():
        for n in range(3):
            weight_slice(n).wait_recv()
            begin(weight_half, n)

    def own_sum(n):
        if n == 0:
            at = pl.multiple_of(cols_of(0, 0), COLS)
            own[...] = jnp.dot(att[pl.ds(0, NEAR)], w[:, pl.ds(at, COLS)], preferred_element_type=jnp.float32)
        else:
            if n == 3:
                att_relay(0).wait_recv()
                att_relay(1).wait_recv()
            weight_half(n - 1).wait_recv()
            own[...] += jnp.dot(gathered[n - 1], slices[n - 1], preferred_element_type=jnp.float32)

    def w_mid(g, i):
        at = w_rows(g)
        w_far(g, i).wait_recv()
        part[i, 0, at] = (wide(part[i, 0, at]) + wide(wx[g, i, :X_ROWS[g]])).astype(jnp.bfloat16)
        if i == 2:
            begin(w_near, g, 0, 0)
            begin(w_near, g, 1, 0)
        else:
            begin(w_near, g, (1 if i == 3 else 0), 1)

    def w_add(g, way):
        add_half(w_near, 0, w_rows(g), lambda: wy[g, way, 0, :X_ROWS[g]], g, way)

    def w_out(g):
        at, size = w_rows(g), X_ROWS[g]
        w_far(g, 0).wait_recv()
        both_ways(w_near, g)
        total = wide(part[0, 0, at]) + wide(wx[g, 0, :size]) + came_along_y(wy, g, size)
        out_ref[at] = total.astype(jnp.bfloat16)

    def find_pages():
        lanes = lax.broadcasted_iota(jnp.int32, (8, 128), 1)

        def look(i, carry):
            found, count = carry
            mine = owner_ref[i] == grp
            found = jnp.where((lanes == count) & mine, i, found)
            return found, count + jnp.where(mine, 1, 0)

        found, count = lax.fori_loop(0, NPAGES, look, (jnp.zeros((8, 128), jnp.int32), 0 * grp), unroll=8)
        table_v[...] = found
        fetch = pltpu.make_async_copy(table_v, table_s, load_sem.at[5])
        fetch.start()
        fetch.wait()
        return count

    def hand_pages(first, count):
        @pl.loop(first, first + SLOTS // 4)
        def _(s):
            page = table_s[0, s]
            slot = place[page // 8]
            rows = kv[slot * 8 + lax.rem(page, 8)]
            pages_ref[s] = jnp.where(s < count, rows, jnp.zeros_like(rows))

    owned = 0
    for step, *which in ORDER:
        if step == "p":
            project(*which)
        elif step in ("sa", "sn", "sx"):
            begin({"sa": att_rows, "sn": u_near, "sx": w_far}[step], *which)
        elif step == "pages":
            if which[0] == 0:
                owned = find_pages()
            hand_pages(which[0] * (SLOTS // 4), owned)
        else:
            {"na": u_add, "nc": u_cross, "no": u_out, "wm": w_mid, "wa": w_add, "wo": w_out,
             "forward": forward, "relay": relay, "sum": own_sum}[step](*which)

    for make, which in sent:
        make(*which).wait_send()


def on_device(queries, key_rows, value_rows, out_weight, block_order, page_owner):
    dma = pltpu.SemaphoreType.DMA
    vmem = pltpu.VMEM
    bf16, f32, i32 = jnp.bfloat16, jnp.float32, jnp.int32
    hbm = pl.BlockSpec(memory_space=pltpu.HBM)
    vmem_out = pl.BlockSpec(memory_space=pltpu.VMEM)
    made = pl.pallas_call(
        kernel,
        name="attend",
        out_shape=(vmem((ROWS, COLS), bf16), vmem((SLOTS, PAGE, 2 * HEAD), bf16)),
        in_specs=[hbm] * 6,
        out_specs=(vmem_out, vmem_out),
        scratch_shapes=[
            vmem((3, QPK * HEAD, COLS), bf16),
            vmem((3, NEAR, QPK * HEAD), bf16),
            vmem((NEAR, COLS), f32),
            pltpu.SMEM((32,), i32),
            pltpu.SMEM((NPAGES,), i32),
            vmem((NPAGES, PAGE, 2 * HEAD), bf16),
            vmem((ROWS, QPK * HEAD), bf16),
            vmem((QPK, ROWS, 2 * HEAD), bf16),
            vmem((QPK, ROWS, HEAD), f32),
            vmem((QPK, ROWS, 2 * HEAD), f32),
            vmem((ROWS, QPK * HEAD), bf16),
            vmem((QPK * HEAD, 8 * COLS), bf16),
            vmem((4, 2, ROWS, COLS), bf16),
            vmem((Y_FIRST, 2, 3, max(Y_ROWS), COLS // 2), bf16),
            vmem((Y_FIRST, max(Y_ROWS), COLS), bf16),
            vmem((X_FIRST, 4, max(X_ROWS), COLS), bf16),
            vmem((X_FIRST, 2, 3, max(X_ROWS), COLS // 2), bf16),
            vmem((8, 128), i32),
            pltpu.SMEM((8, 128), i32),
            pltpu.SMEM((64,), i32),
            pltpu.SMEM((64,), i32),
            dma((8,)), dma,
            dma((2, 11)), dma((2, 11)), dma((8,)), dma((8,)), dma((N_SET,)), dma((N_SET,)),
            dma((3,)), dma((3,)), dma((3,)), dma((3,)), dma((4,)), dma((4,)),
            dma((Y_FIRST, 2, 3)), dma((Y_FIRST, 2, 3)), dma((Y_FIRST,)), dma((Y_FIRST,)),
            dma((X_FIRST, 4)), dma((X_FIRST, 4)), dma((X_FIRST, 2, 3)), dma((X_FIRST, 2, 3)),
        ],
        compiler_params=pltpu.CompilerParams(
            collective_id=0, has_side_effects=True, vmem_limit_bytes=56 * 2**20),
    )(block_order, page_owner.reshape(NPAGES), queries,
      key_rows.reshape(PAGE, PAGE, HEAD), value_rows.reshape(PAGE, PAGE, HEAD), out_weight)
    return made


def solution(mesh):
    placed = (P("grp", "tp"), P("grp", "tp"), P("grp", "tp"), P("tp", None), P(), P())
    return jax.shard_map(
        on_device,
        mesh=mesh,
        in_specs=placed,
        out_specs=(P("grp", "tp"), P("grp", None, "tp")),
        check_vma=False,
    )
```

```python
import functools

import jax
import jax.numpy as jnp
from jax import lax
from jax.experimental import pallas as pl
from jax.experimental.pallas import tpu as pltpu
from jax.sharding import PartitionSpec as P

MESH = pl.DeviceIdType.MESH
HEAD = 128
QPK = 4
ROWS = 256
PAGE = 16
COLS = 1024
SLOTS = 64
NPAGES = 512
NEG = -1e30
SCALE2 = 128.0 ** -0.5 * 1.4426950408889634

Z_SET = (1, 3, 4, 5, 7, 8, 9, 10, 12, 13, 15)
X_SET = (2, 6, 11, 14)
N_SET = 16

Y_ROWS = (64, 64, 32)
X_ROWS = (48, 48)
Y_FIRST, X_FIRST = len(Y_ROWS), len(X_ROWS)
NEAR = sum(Y_ROWS)
ORDER = (
    ("sa", 0), ("sa", 1),
    ("p", 2, 1), ("sn", 0, 0, 0), ("sn", 0, 1, 0), ("sx", 0, 2), ("p", 1, 1), ("sn", 0, 0, 1),
    ("sn", 1, 0, 0), ("sn", 1, 0, 1), ("sn", 2, 0, 0), ("sn", 2, 0, 1), ("sx", 0, 1), ("p", 3, 1),
    ("sn", 0, 1, 1), ("sn", 1, 1, 0), ("sn", 1, 1, 1), ("sn", 2, 1, 0), ("sn", 2, 1, 1),
    ("sx", 0, 3), ("p", 0, 1), ("sx", 0, 0), ("sx", 1, 2), ("sx", 1, 1), ("sx", 1, 3), ("sx", 1, 0),
    ("p", 2, 0), ("p", 1, 0), ("p", 3, 0), ("p", 0, 0), ("forward",), ("pages", 0), ("pages", 1), ("wm", 0, 2),
    ("relay", 0), ("relay", 1), ("na", 0, 0), ("na", 0, 1), ("pages", 2), ("pages", 3), ("wm", 0, 1), ("sum", 0), ("wm", 0, 3),
    ("na", 1, 0), ("na", 1, 1), ("sum", 1), ("sum", 2), ("wm", 1, 2), ("na", 2, 0), ("na", 2, 1),
    ("wa", 0, 0), ("wa", 0, 1), ("wm", 1, 1), ("nc", 0), ("sum", 3), ("wm", 1, 3), ("nc", 1), ("wa", 1, 0), ("wa", 1, 1),
    ("nc", 2), ("wo", 0), ("no", 0), ("wo", 1), ("no", 1), ("no", 2),
)


def plus_slot(r):
    return 4 * Z_SET[r]


def minus_slot(r):
    return 4 * Z_SET[r] + 1


def x_slot(i):
    return 4 * X_SET[i // 2] + i % 2


def half_blocks(z, xl, c):
    def index(dz, other, flip):
        return lax.rem(z + dz + 8, 8) * 4 + (1 - xl if other else xl) * 2 + (1 - c if flip else c)

    found = []
    for flip in (0, 1):
        at = 2 * flip
        found += [(at, index(0, 0, flip), 0), (at + 1, index(0, 0, flip), 1)]
        for r in range(11):
            d = r // 3 + 1
            if r < 9:
                half, other = ((0, 0), (1, 0), (0, 1))[r % 3]
            else:
                half, other = (0, r - 9)
            found.append((plus_slot(r) + at, index(-d, other, flip), half))
            if r < 9:
                half, other = ((1, 0), (0, 0), (0, 1))[r % 3]
            else:
                half, other = (1, r - 9)
            found.append((minus_slot(r) + at, index(d, other, flip), half))
        for i, (dz, half) in enumerate(((0, 0), (0, 1), (1, 1), (-1, 1), (2, 1), (-2, 1), (3, 1), (-3, 1))):
            found.append((x_slot(i) + at, index(dz, 1, flip), half))
    return found


def kernel(order_hbm, owner_hbm, q_hbm, k_hbm, v_hbm, w_hbm, out_ref, pages_ref,
           slices, gathered, own, order_ref, owner_ref, kv, q_raw, qx, top, acc, att, w, part, uy, ux, wx, wy, table_v, table_s, place, holder,
           load_sem, w_sem, z_ssem, z_rsem, x_ssem, x_rsem, d_ssem, d_rsem,
           slice_ssem, slice_rsem, half_ssem, half_rsem, att_ssem, att_rsem,
           uy_ssem, uy_rsem, ux_ssem, ux_rsem, wx_ssem, wx_rsem, wy_ssem, wy_rsem):
    grp, tp = lax.axis_index("grp"), lax.axis_index("tp")
    z, xl, c = grp // 4, lax.rem(grp // 2, 2), lax.rem(grp, 2)
    y, xh = tp // 2, lax.rem(tp, 2)

    def at_grp(z_to, xl_to, c_to):
        return (z_to * 4 + xl_to * 2 + c_to, tp)

    z_up = at_grp(lax.rem(z + 1, 8), xl, c)
    z_down = at_grp(lax.rem(z + 7, 8), xl, c)
    x_near = at_grp(z, 1 - xl, c)
    core = at_grp(z, xl, 1 - c)
    y_up = (grp, lax.rem(y + 1, 4) * 2 + xh)
    y_down = (grp, lax.rem(y + 3, 4) * 2 + xh)
    y_far = (grp, lax.rem(y + 2, 4) * 2 + xh)
    x_far = (grp, y * 2 + 1 - xh)

    barrier = pltpu.get_barrier_semaphore()
    for near in (z_up, z_down, x_near, core, y_up, y_down, y_far, x_far):
        pl.semaphore_signal(barrier, inc=1, device_id=near, device_id_type=MESH)

    loads = []
    for half in range(2):
        for ref, lane in ((k_hbm, 0), (v_hbm, HEAD)):
            loads.append(pltpu.make_async_copy(
                ref.at[pl.ds(8 * half, 8)], kv.at[pl.ds(8 * half, 8), :, pl.ds(lane, HEAD)],
                load_sem.at[len(loads)]))
    load_q = pltpu.make_async_copy(q_hbm, q_raw, load_sem.at[4])
    load_w = pltpu.make_async_copy(w_hbm, w, w_sem)
    for load in loads:
        load.start()
    load_order = pltpu.make_async_copy(order_hbm, order_ref, load_sem.at[6])
    load_owner = pltpu.make_async_copy(owner_hbm, owner_ref, load_sem.at[7])
    load_order.start()
    load_owner.start()
    load_q.start()
    load_w.start()

    for slot, block, half in half_blocks(z, xl, c):
        place[2 * block + half] = slot + 0 * grp
        holder[slot] = block

    for load in loads:
        load.wait()
    pl.semaphore_wait(barrier, 8)

    sent = []

    def remote(src, dst, ssem, rsem, to):
        return pltpu.make_async_remote_copy(src_ref=src, dst_ref=dst, send_sem=ssem, recv_sem=rsem,
                                            device_id=to, device_id_type=MESH)

    def slots(first, count=1):
        return kv.at[pl.ds(8 * first, 8 * count)]

    def plus(r, src):
        return remote(slots(src), slots(plus_slot(r)), z_ssem.at[0, r], z_rsem.at[0, r], z_up)

    def minus(r, src):
        return remote(slots(src), slots(minus_slot(r)), z_ssem.at[1, r], z_rsem.at[1, r], z_down)

    def cross(i, src):
        return remote(slots(src), slots(x_slot(i)), x_ssem.at[i], x_rsem.at[i], x_near)

    def twin(k):
        return remote(slots(4 * k, 2), slots(4 * k + 2, 2), d_ssem.at[k], d_rsem.at[k], core)

    def begin(make, *which):
        make(*which).start()
        sent.append((make, which))

    begin(cross, 0, 0)
    begin(plus, 0, 0)
    begin(minus, 0, 1)
    begin(twin, 0)
    begin(cross, 1, 1)
    begin(plus, 1, 1)
    begin(minus, 1, 0)

    ahead = (y_up, y_down, y_far)
    steps = (1, 3, 2)

    def weight_slice(n):
        first = (lax.rem(y + steps[n], 4) * 2 + xh) * COLS
        src = w_hbm.at[pl.ds(pl.multiple_of(256 * c, 256), 256), pl.ds(pl.multiple_of(first, COLS), COLS)]
        return remote(src, slices.at[n, pl.ds(pl.multiple_of(256 * c, 256), 256)],
                      slice_ssem.at[n], slice_rsem.at[n], ahead[n])

    def weight_half(n):
        half = slices.at[n, pl.ds(pl.multiple_of(256 * c, 256), 256)]
        return remote(half, half, half_ssem.at[n], half_rsem.at[n], core)

    for n in range(3):
        begin(weight_slice, n)

    def z_step(r):
        plus(r, 0).wait_recv()
        minus(r, 0).wait_recv()
        if r <= 6:
            begin(plus, r + 3, plus_slot(r))
            begin(minus, r + 3, minus_slot(r))
        if r == 8:
            begin(plus, 10, plus_slot(8))
        if r % 3 == 0 and r <= 6:
            begin(cross, 2 + 2 * (r // 3), minus_slot(r))
        if r % 3 == 1 and r <= 7:
            begin(cross, 3 + 2 * (r // 3), plus_slot(r))
        begin(twin, Z_SET[r])

    def x_step(i):
        cross(i, 0).wait_recv()
        if i == 0:
            begin(plus, 2, x_slot(0))
            begin(minus, 2, x_slot(0))
        if i == 6:
            begin(minus, 10, x_slot(6))
        if i % 2 == 1:
            begin(twin, X_SET[i // 2])

    before = {
        1: (("x", 0), ("z", 0), ("x", 1), ("z", 1)),
        3: (("z", 2), ("x", 2)),
        4: (("z", 3), ("x", 3)),
        5: (("z", 4),),
        6: (("z", 5),),
        7: (("z", 6), ("x", 4)),
        8: (("x", 5), ("z", 7)),
        10: (("z", 8), ("x", 6)),
        11: (("z", 9),),
        12: (("x", 7),),
        13: (("z", 10),),
    }

    def softmax_step(k, first):
        block = kv[pl.ds(32 * k, 32)].reshape(512, 2 * HEAD)
        rows = []
        for j in range(4):
            seen = order_ref[holder[4 * k + j]] < here
            if first and j < 2:
                seen = True
            rows.append(jnp.full((HEAD, HEAD), jnp.where(seen, 0.0, NEG), jnp.float32).astype(jnp.bfloat16))
        keys = jnp.concatenate([block[:, :HEAD], jnp.concatenate(rows, axis=0)], axis=1)
        values = jnp.concatenate([block[:, HEAD:], jnp.ones((512, HEAD), jnp.bfloat16)], axis=1)
        scores = [lax.dot_general(qx[h], keys, (((1,), (1,)), ((), ())), preferred_element_type=jnp.float32)
                  for h in range(QPK)]
        for h in range(QPK):
            tiles = [scores[h][:, HEAD * j:HEAD * (j + 1)] for j in range(4)]
            if first:
                row = lax.broadcasted_iota(jnp.int32, (ROWS, HEAD), 0)
                lane = lax.broadcasted_iota(jnp.int32, (ROWS, HEAD), 1)
                for j in range(2):
                    tiles[j] = jnp.where(lane + HEAD * j <= row, tiles[j], NEG)
            peak = jnp.max(jnp.maximum(jnp.maximum(tiles[0], tiles[1]), jnp.maximum(tiles[2], tiles[3])),
                           axis=1, keepdims=True)
            if first:
                new = jnp.broadcast_to(peak, (ROWS, HEAD))
            else:
                old = top[h]
                new = jnp.maximum(old, peak)
            expo = [jnp.exp2((tile - new) * SCALE2).astype(jnp.bfloat16) for tile in tiles]
            gained = jnp.dot(jnp.concatenate(expo, axis=1), values, preferred_element_type=jnp.float32)
            top[h] = new
            if first:
                acc[h] = gained
            else:
                factor = jnp.exp2((old - new) * SCALE2)
                acc[h] = acc[h] * jnp.concatenate([factor, factor], axis=1) + gained

    load_order.wait()
    load_owner.wait()
    here = order_ref[grp]
    load_q.wait()
    lane = lax.broadcasted_iota(jnp.int32, (ROWS, HEAD), 1)
    unit = jnp.where(lane == 0, 1.0, 0.0).astype(jnp.bfloat16)
    for h in range(QPK):
        qx[h] = jnp.concatenate([q_raw[:, HEAD * h:HEAD * (h + 1)], unit], axis=1)
    twin(0).wait_recv()
    softmax_step(0, True)

    @pl.loop(1, N_SET)
    def _(k):
        for at, events in before.items():
            @pl.when(k == at)
            def _():
                for kind, r in events:
                    (z_step if kind == "z" else x_step)(r)
        twin(k).wait_recv()
        softmax_step(k, False)

    for h in range(QPK):
        att[:, HEAD * h:HEAD * (h + 1)] = (acc[h, :, :HEAD] / acc[h, :, HEAD:]).astype(jnp.bfloat16)
    load_w.wait()

    def cols_of(i, j):
        return (lax.rem(y + i, 4) * 2 + (1 - xh if j else xh)) * COLS

    def project(i, j):
        rows = pl.ds(0, ROWS) if j else pl.ds(NEAR, ROWS - NEAR)
        for n in range(2):
            at = pl.multiple_of(cols_of(i, j) + n * 512, 512)
            part[i, j, rows, pl.ds(n * 512, 512)] = jnp.dot(
                att[rows], w[:, pl.ds(at, 512)], preferred_element_type=jnp.float32).astype(jnp.bfloat16)

    def u_rows(g):
        return pl.ds(sum(Y_ROWS[:g]), Y_ROWS[g])

    def w_rows(g):
        return pl.ds(NEAR + sum(X_ROWS[:g]), X_ROWS[g])

    def att_rows(n):
        return remote(att.at[pl.ds(0, NEAR)], gathered.at[n], att_ssem.at[n], att_rsem.at[n], ahead[n])

    def att_relay(way):
        half = pl.ds(NEAR // 2 * way, NEAR // 2)
        return remote(gathered.at[way, half], gathered.at[2, half], att_ssem.at[2 + way], att_rsem.at[2 + way],
                      ahead[way])

    def relay(way):
        att_rows(way).wait_recv()
        begin(att_relay, way)

    def along_y(way, n, j, rows, to, ssem, rsem):
        i = (2, 1, 1)[n] if way == 0 else (2, 3, 3)[n]
        left = (0, 1, 0)[n] if way == 0 else (1, 0, 1)[n]
        return remote(part.at[i, j, rows, pl.ds(512 * left, 512)], to, ssem, rsem, (y_up, y_down)[way])

    def u_near(g, way, n):
        return along_y(way, n, 1, u_rows(g), uy.at[g, way, n, pl.ds(0, Y_ROWS[g])],
                       uy_ssem.at[g, way, n], uy_rsem.at[g, way, n])

    def w_near(g, way, n):
        return along_y(way, n, 0, w_rows(g), wy.at[g, way, n, pl.ds(0, X_ROWS[g])],
                       wy_ssem.at[g, way, n], wy_rsem.at[g, way, n])

    def u_far(g):
        return remote(part.at[0, 1, u_rows(g)], ux.at[g, pl.ds(0, Y_ROWS[g])], ux_ssem.at[g], ux_rsem.at[g], x_far)

    def w_far(g, i):
        return remote(part.at[i, 1, w_rows(g)], wx.at[g, i, pl.ds(0, X_ROWS[g])],
                      wx_ssem.at[g, i], wx_rsem.at[g, i], x_far)

    def wide(a):
        return a.astype(jnp.float32)

    def add_half(near, j, rows, came, g, way):
        i, cols = (1, 3)[way], pl.ds(512 * way, 512)
        near(g, way, 0).wait_recv()
        part[i, j, rows, cols] = (wide(part[i, j, rows, cols]) + wide(came())).astype(jnp.bfloat16)
        begin(near, g, way, 2)

    def both_ways(near, g):
        for way in (0, 1):
            for n in (1, 2):
                near(g, way, n).wait_recv()

    def came_along_y(buf, g, size):
        return jnp.concatenate([wide(buf[g, 0, 2 - left, :size]) + wide(buf[g, 1, 1 + left, :size])
                                for left in (0, 1)], axis=1)

    def u_add(g, way):
        add_half(u_near, 1, u_rows(g), lambda: uy[g, way, 0, :Y_ROWS[g]], g, way)

    def u_cross(g):
        both_ways(u_near, g)
        part[0, 1, u_rows(g)] = (wide(part[0, 1, u_rows(g)]) + came_along_y(uy, g, Y_ROWS[g])).astype(jnp.bfloat16)
        begin(u_far, g)

    def u_out(g):
        u_far(g).wait_recv()
        out_ref[u_rows(g)] = (own[u_rows(g)] + wide(ux[g, :Y_ROWS[g]])).astype(jnp.bfloat16)

    def forward():
        for n in range(3):
            weight_slice(n).wait_recv()
            begin(weight_half, n)

    def own_sum(n):
        if n == 0:
            at = pl.multiple_of(cols_of(0, 0), COLS)
            own[...] = jnp.dot(att[pl.ds(0, NEAR)], w[:, pl.ds(at, COLS)], preferred_element_type=jnp.float32)
        else:
            if n == 3:
                att_relay(0).wait_recv()
                att_relay(1).wait_recv()
            weight_half(n - 1).wait_recv()
            own[...] += jnp.dot(gathered[n - 1], slices[n - 1], preferred_element_type=jnp.float32)

    def w_mid(g, i):
        at = w_rows(g)
        w_far(g, i).wait_recv()
        part[i, 0, at] = (wide(part[i, 0, at]) + wide(wx[g, i, :X_ROWS[g]])).astype(jnp.bfloat16)
        if i == 2:
            begin(w_near, g, 0, 0)
            begin(w_near, g, 1, 0)
        else:
            begin(w_near, g, (1 if i == 3 else 0), 1)

    def w_add(g, way):
        add_half(w_near, 0, w_rows(g), lambda: wy[g, way, 0, :X_ROWS[g]], g, way)

    def w_out(g):
        at, size = w_rows(g), X_ROWS[g]
        w_far(g, 0).wait_recv()
        both_ways(w_near, g)
        total = wide(part[0, 0, at]) + wide(wx[g, 0, :size]) + came_along_y(wy, g, size)
        out_ref[at] = total.astype(jnp.bfloat16)

    def find_pages():
        lanes = lax.broadcasted_iota(jnp.int32, (8, 128), 1)

        def look(i, carry):
            found, count = carry
            mine = owner_ref[i] == grp
            found = jnp.where((lanes == count) & mine, i, found)
            return found, count + jnp.where(mine, 1, 0)

        found, count = lax.fori_loop(0, NPAGES, look, (jnp.zeros((8, 128), jnp.int32), 0 * grp), unroll=8)
        table_v[...] = found
        fetch = pltpu.make_async_copy(table_v, table_s, load_sem.at[5])
        fetch.start()
        fetch.wait()
        return count

    def hand_pages(first, count):
        @pl.loop(first, first + SLOTS // 4)
        def _(s):
            page = table_s[0, s]
            slot = place[page // 8]
            rows = kv[slot * 8 + lax.rem(page, 8)]
            pages_ref[s] = jnp.where(s < count, rows, jnp.zeros_like(rows))

    owned = 0
    for step, *which in ORDER:
        if step == "p":
            project(*which)
        elif step in ("sa", "sn", "sx"):
            begin({"sa": att_rows, "sn": u_near, "sx": w_far}[step], *which)
        elif step == "pages":
            if which[0] == 0:
                owned = find_pages()
            hand_pages(which[0] * (SLOTS // 4), owned)
        else:
            {"na": u_add, "nc": u_cross, "no": u_out, "wm": w_mid, "wa": w_add, "wo": w_out,
             "forward": forward, "relay": relay, "sum": own_sum}[step](*which)

    for make, which in sent:
        make(*which).wait_send()


def on_device(queries, key_rows, value_rows, out_weight, block_order, page_owner):
    dma = pltpu.SemaphoreType.DMA
    vmem = pltpu.VMEM
    bf16, f32, i32 = jnp.bfloat16, jnp.float32, jnp.int32
    hbm = pl.BlockSpec(memory_space=pltpu.HBM)
    vmem_out = pl.BlockSpec(memory_space=pltpu.VMEM)
    made = pl.pallas_call(
        kernel,
        name="attend",
        out_shape=(vmem((ROWS, COLS), bf16), vmem((SLOTS, PAGE, 2 * HEAD), bf16)),
        in_specs=[hbm] * 6,
        out_specs=(vmem_out, vmem_out),
        scratch_shapes=[
            vmem((3, QPK * HEAD, COLS), bf16),
            vmem((3, NEAR, QPK * HEAD), bf16),
            vmem((NEAR, COLS), f32),
            pltpu.SMEM((32,), i32),
            pltpu.SMEM((NPAGES,), i32),
            vmem((NPAGES, PAGE, 2 * HEAD), bf16),
            vmem((ROWS, QPK * HEAD), bf16),
            vmem((QPK, ROWS, 2 * HEAD), bf16),
            vmem((QPK, ROWS, HEAD), f32),
            vmem((QPK, ROWS, 2 * HEAD), f32),
            vmem((ROWS, QPK * HEAD), bf16),
            vmem((QPK * HEAD, 8 * COLS), bf16),
            vmem((4, 2, ROWS, COLS), bf16),
            vmem((Y_FIRST, 2, 3, max(Y_ROWS), COLS // 2), bf16),
            vmem((Y_FIRST, max(Y_ROWS), COLS), bf16),
            vmem((X_FIRST, 4, max(X_ROWS), COLS), bf16),
            vmem((X_FIRST, 2, 3, max(X_ROWS), COLS // 2), bf16),
            vmem((8, 128), i32),
            pltpu.SMEM((8, 128), i32),
            pltpu.SMEM((64,), i32),
            pltpu.SMEM((64,), i32),
            dma((8,)), dma,
            dma((2, 11)), dma((2, 11)), dma((8,)), dma((8,)), dma((N_SET,)), dma((N_SET,)),
            dma((3,)), dma((3,)), dma((3,)), dma((3,)), dma((4,)), dma((4,)),
            dma((Y_FIRST, 2, 3)), dma((Y_FIRST, 2, 3)), dma((Y_FIRST,)), dma((Y_FIRST,)),
            dma((X_FIRST, 4)), dma((X_FIRST, 4)), dma((X_FIRST, 2, 3)), dma((X_FIRST, 2, 3)),
        ],
        compiler_params=pltpu.CompilerParams(
            collective_id=0, has_side_effects=True, vmem_limit_bytes=56 * 2**20),
    )(block_order, page_owner.reshape(NPAGES), queries,
      key_rows.reshape(PAGE, PAGE, HEAD), value_rows.reshape(PAGE, PAGE, HEAD), out_weight)
    return made


def solution(mesh):
    placed = (P("grp", "tp"), P("grp", "tp"), P("grp", "tp"), P("tp", None), P(), P())
    return jax.shard_map(
        on_device,
        mesh=mesh,
        in_specs=placed,
        out_specs=(P("grp", "tp"), P("grp", None, "tp")),
        check_vma=False,
    )
```
